256 devices in a mesh: outer: 4 (over z_hi), inner: 16 (over z_lo, x, core), head: 4 (over y).
Axes of the slice: x: 4, y: 4, z: 8 (z_hi: 4, z_lo: 2; z = z_hi * 2 + z_lo), core: 2. Of those that a mesh axis runs over, the one named last changes fastest.
Arguments:
- queries: bfloat16 [65536, 1024], P(('outer', 'inner'), 'head'), may hold values from -10 to 10
- keys: bfloat16 [65536, 128], P(('outer', 'inner', 'head')), may hold values from -10 to 10
- values: bfloat16 [65536, 128], P(('outer', 'inner', 'head')), may hold values from -6 to 6
- doc_lengths: int32 [28], replicated, may hold values from 1 to 3584, as said below
- block_count: int32 [64], replicated, may hold values from 1 to 2, as said below
Outputs:
- attended: bfloat16 [65536, 1024], P(('outer', 'inner'), 'head')
The draws below stay inside these ranges and needn't reach their ends.
Inputs may be any that keep to these rules, and one draw needn't show every extreme that they name: `doc_lengths`: the lengths sum to 49152, and one rollout has exactly 3584 tokens. `block_count`: exactly half of the 64 context devices hold 2 blocks and the others 1; where 64 >= 16, 8 consecutive context devices hold 1 block each; the blocks follow one another in device order.
All inputs are finite; a program needn't handle non-finite values.
Results may differ from the reference program's by a relative error of at most 0.0032.
Values may be sent and summed in bfloat16 or wider, within the bound.
A program may use at most 64 MiB of HBM per device.

```python
import math
import jax
import jax.numpy as jnp
from jax import lax

HEAD_DIM = 128
GROUP_HEADS = 8
BLOCK = 512
SLOTS = 2
REACH = 7
CONTEXT = 64
NBLOCKS = 96
TOKENS = 49152
ROWS = 65536
LONGEST = 3584
DOCUMENTS = 28


def draw_queries(key, part):
    noise_key = jax.random.fold_in(key, 3)
    base = jnp.clip(1.5 * jax.random.normal(noise_key, (ROWS, GROUP_HEADS * HEAD_DIM), jnp.float32), -9.0, 9.0)
    return base.astype(jnp.bfloat16)


def draw_keys(key, part):
    noise_key = jax.random.fold_in(key, 5)
    base = jnp.clip(1.5 * jax.random.normal(noise_key, (ROWS, HEAD_DIM), jnp.float32), -9.0, 9.0)
    return base.astype(jnp.bfloat16)


def pack_layout(key):
    base_key = jax.random.fold_in(key, 31)
    run_key, shuffle_key, offset_key, jitter_key = jax.random.split(base_key, 4)
    device_index = jnp.arange(CONTEXT, dtype=jnp.int32)
    if CONTEXT >= 2 * (REACH + 1):
        run_length = REACH + 1
        run_start = jax.random.randint(run_key, (), 0, CONTEXT - run_length + 1, dtype=jnp.int32)
        shuffled = jax.random.permutation(shuffle_key, CONTEXT - run_length)
        others = (1 + (shuffled < CONTEXT // 2).astype(jnp.int32)).astype(jnp.int32)
        in_run = (device_index >= run_start) & (device_index < run_start + run_length)
        other_index = jnp.where(device_index < run_start, device_index, device_index - run_length)
        other_index = jnp.clip(other_index, 0, CONTEXT - run_length - 1)
        counts = jnp.where(in_run, 1, others[other_index]).astype(jnp.int32)
        blocks_before = jnp.sum(jnp.where(device_index < run_start, counts, 0)).astype(jnp.int32)
        first_block = jnp.minimum(blocks_before, NBLOCKS - REACH - 1)
    else:
        shuffled = jax.random.permutation(shuffle_key, CONTEXT)
        counts = (1 + (shuffled < CONTEXT // 2).astype(jnp.int32)).astype(jnp.int32)
        first_block = jnp.zeros((), jnp.int32)
    offset = jax.random.randint(offset_key, (), BLOCK // 4, BLOCK - BLOCK // 4, dtype=jnp.int32)
    return (counts, (first_block * BLOCK + offset).astype(jnp.int32), jitter_key)


def cut_points(total, count, raw, others):
    index = jnp.arange(others + 1, dtype=jnp.int32)
    safe = jnp.maximum(count, 1)
    low = total // safe
    high = (total + safe - 1) // safe
    spread = jnp.maximum(jnp.minimum(low // 4, (LONGEST - high) // 2), 0)
    jitter = raw % (2 * spread + 1) - spread
    inside = (index > 0) & (index < count)
    return index * total // safe + jnp.where(inside, jitter, 0)


def draw_doc_lengths(key, part):
    counts, before, jitter_key = pack_layout(key)
    others = DOCUMENTS - 1
    after = TOKENS - LONGEST - before
    lead = jnp.clip(before * others // (before + after), (before + LONGEST - 1) // LONGEST, others - (after + LONGEST - 1) // LONGEST).astype(jnp.int32)
    trail = (others - lead).astype(jnp.int32)
    lead_key, trail_key = jax.random.split(jitter_key, 2)
    lead_raw = jax.random.randint(lead_key, (others + 1,), 0, 1 << 20, dtype=jnp.int32)
    trail_raw = jax.random.randint(trail_key, (others + 1,), 0, 1 << 20, dtype=jnp.int32)
    lead_cuts = cut_points(before, lead, lead_raw, others)
    trail_cuts = cut_points(after, trail, trail_raw, others)
    lead_sizes = lead_cuts[1:] - lead_cuts[:-1]
    trail_sizes = trail_cuts[1:] - trail_cuts[:-1]
    slot = jnp.arange(DOCUMENTS, dtype=jnp.int32)
    lead_pick = lead_sizes[jnp.clip(slot, 0, others - 1)]
    trail_pick = trail_sizes[jnp.clip(slot - lead - 1, 0, others - 1)]
    lengths = jnp.where(slot < lead, lead_pick, jnp.where(slot == lead, LONGEST, trail_pick))
    return lengths.astype(jnp.int32)


def draw_block_count(key, part):
    counts, before, jitter_key = pack_layout(key)
    return counts


def levels(key, shape, shards, least, largest):
    def one(dim, blocks):
        draws = jax.random.uniform(jax.random.fold_in(jax.random.fold_in(key, 6), dim), (blocks,), jnp.float32, least / len(shards), largest / len(shards))
        return jnp.repeat(jnp.exp(draws), shape[dim] // blocks).reshape((-1,) + (1,) * (len(shape) - dim - 1))

    loudness = one(*shards[0])
    for cut in shards[1:]:
        loudness = loudness * one(*cut)
    return loudness


def scatter_about(key, shape, deviation, limit, cuts=(), kind=jnp.bfloat16):
    level = levels(key, shape, cuts, -0.22, 0.18) if cuts else 1.0
    values = jax.random.normal(key, shape, jnp.float32) * deviation * level
    return jnp.minimum(jnp.maximum(values, -limit), limit).astype(kind)


def setup_inputs(seed: int = 0) -> dict:
    arg_keys = jax.random.split(jax.random.key(seed), 6)
    queries = draw_queries(jax.random.fold_in(arg_keys[5], 71), 0)
    keys = draw_keys(jax.random.fold_in(arg_keys[5], 71), 0)
    values = scatter_about(arg_keys[2], (ROWS, HEAD_DIM), 1.0, 6.0, ((0, 256),))
    doc_lengths = draw_doc_lengths(jax.random.fold_in(arg_keys[5], 71), 0)
    block_count = draw_block_count(jax.random.fold_in(arg_keys[5], 71), 0)
    return dict(queries=queries, keys=keys, values=values, doc_lengths=doc_lengths, block_count=block_count)


NEGATIVE = -1e+30

def reference(queries, keys, values, doc_lengths, block_count):
    block_rows = SLOTS * BLOCK
    context = block_count.shape[0]
    starts = ((jnp.cumsum(block_count) - block_count) * BLOCK).astype(jnp.int32)
    offsets = jnp.arange(block_rows, dtype=jnp.int32)
    position = (starts[:, None] + offsets[None, :]).astype(jnp.int32)
    is_live = offsets[None, :] < (block_count * BLOCK)[:, None]
    bounds = jnp.cumsum(doc_lengths).astype(jnp.int32)
    doc_ids = lax.optimization_barrier(jnp.sum((position[:, :, None] >= bounds[None, None, :]).astype(jnp.int32), axis=2)).astype(jnp.int32)

    def padded(array, fill):
        front = jnp.full((REACH,) + array.shape[1:], fill, array.dtype)
        return jnp.concatenate([front, array], axis=0)
    key_units = padded(keys.reshape(context, block_rows, HEAD_DIM), 0)
    value_units = padded(values.reshape(context, block_rows, HEAD_DIM), 0)
    pos_units = padded(position, 0)
    live_units = padded(is_live, False)
    doc_units = padded(doc_ids, -1)
    query_units = queries.reshape(context, block_rows, GROUP_HEADS, HEAD_DIM)
    score_scale = 1.0 / math.sqrt(HEAD_DIM)

    def one_device(index):

        def window_of(array):
            taken = lax.dynamic_slice_in_dim(array, index, REACH + 1, 0)
            return taken.reshape((-1,) + array.shape[2:])
        key_rows = window_of(key_units).astype(jnp.float32)
        value_rows = window_of(value_units).astype(jnp.float32)
        key_pos = window_of(pos_units)
        key_live = window_of(live_units)
        key_doc = window_of(doc_units)
        query_rows = lax.dynamic_index_in_dim(query_units, index, 0, keepdims=False).astype(jnp.float32)
        own_pos = lax.dynamic_index_in_dim(position, index, 0, keepdims=False)
        own_live = lax.dynamic_index_in_dim(is_live, index, 0, keepdims=False)
        own_doc = lax.dynamic_index_in_dim(doc_ids, index, 0, keepdims=False)
        visible = own_live[:, None] & key_live[None, :] & (own_doc[:, None] == key_doc[None, :]) & (key_pos[None, :] <= own_pos[:, None])
        scores = jnp.einsum('qhd,kd->qhk', query_rows, key_rows) * score_scale
        masked = jnp.where(visible[:, None, :], scores, NEGATIVE)
        row_top = lax.optimization_barrier(jnp.max(masked, axis=2))
        weights = jnp.where(visible[:, None, :], jnp.exp(masked - row_top[:, :, None]), 0.0)
        row_total = lax.optimization_barrier(jnp.sum(weights, axis=2))
        rounded = lax.optimization_barrier(weights.astype(jnp.bfloat16)).astype(jnp.float32)
        weighted = jnp.einsum('qhk,kd->qhd', rounded, value_rows)
        result = jnp.where(own_live[:, None, None], weighted / jnp.where(own_live[:, None], row_total, 1.0)[:, :, None], 0.0)
        return result.astype(jnp.bfloat16)
    outputs = lax.map(one_device, jnp.arange(context, dtype=jnp.int32))
    return outputs.reshape(context * block_rows, GROUP_HEADS * HEAD_DIM)
```

```python
import math

import jax
import jax.numpy as jnp
from jax import lax
from jax.experimental import pallas as pl
from jax.experimental.pallas import tpu as pltpu
from jax.sharding import PartitionSpec as P

BLOCK = 512
SLOTS = 2
REACH = 7
QUARTER = 256
HALF = 128
MESH = pl.DeviceIdType.MESH
NEGATIVE = -1e30


def gather_kernel(k_ref, v_ref, kw, vw, send_sems, recv_sems, local_sems):
    outer = lax.axis_index("outer")
    inner = lax.axis_index("inner")
    y = lax.axis_index("head")
    z = outer * 2 + inner // 8
    x = lax.rem(inner // 2, 4)
    core = lax.rem(inner, 2)

    def place(px, py, pz, pc):
        return (pz // 2, lax.rem(pz, 2) * 8 + px * 2 + pc, py)

    xp, xm = lax.rem(x + 1, 4), lax.rem(x + 3, 4)
    yp, ym = lax.rem(y + 1, 4), lax.rem(y + 3, 4)
    zp, zm = lax.rem(z + 1, 8), lax.rem(z + 7, 8)
    z_next = jnp.where(x == 3, zp, z)
    z_prev = jnp.where(x == 0, zm, z)
    right, left = place(xp, y, z, core), place(xm, y, z, core)
    up, down = place(x, y, zp, core), place(x, y, zm, core)
    after, before = place(x, yp, z, core), place(x, ym, z, core)
    follower, leader = place(xp, y, z_next, core), place(xm, y, z_prev, core)
    sibling = place(x, y, z, 1 - core)

    barrier = pltpu.get_barrier_semaphore()
    for partner in (right, left, up, down, after, before, follower, leader, sibling):
        pl.semaphore_signal(barrier, inc=1, device_id=partner, device_id_type=MESH)

    def rows(order, half=None):
        start = lax.rem(y + order, 4) * QUARTER
        if half is None:
            return pl.ds(pl.multiple_of(start, QUARTER), QUARTER)
        return pl.ds(pl.multiple_of(start + half * HALF, HALF), HALF)

    used = []

    def transfer(src, dst, device, sem=None):
        if sem is None:
            sem = len(used)
            used.append(sem)
        return pltpu.make_async_remote_copy(
            src_ref=src,
            dst_ref=dst,
            send_sem=send_sems.at[sem],
            recv_sem=recv_sems.at[sem],
            device_id=device,
            device_id_type=MESH,
        )

    sent = []

    def go(copy):
        copy.start()
        sent.append(copy)
        return copy

    keep_k = pltpu.make_async_copy(k_ref, kw.at[0, rows(0)], local_sems.at[0])
    keep_v = pltpu.make_async_copy(v_ref, vw.at[0, rows(0)], local_sems.at[1])
    keep_k.start()
    keep_v.start()
    pl.semaphore_wait(barrier, 9)

    def ring_open(src, win, slot):
        return (
            go(transfer(src, win.at[slot, rows(0)], after)),
            go(transfer(src, win.at[slot, rows(0)], before)),
        )

    def ring_pass(win, slot, opened):
        opened[0].wait_recv()
        first = go(transfer(win.at[slot, rows(3, 0)], win.at[slot, rows(3, 0)], after))
        opened[1].wait_recv()
        second = go(transfer(win.at[slot, rows(1, 1)], win.at[slot, rows(1, 1)], before))
        return first, second

    def ring_close(passed):
        passed[0].wait_recv()
        passed[1].wait_recv()

    def climb(src, win, part):
        return go(transfer(src, win.at[8, part], up))

    class Sideways:
        def __init__(self, win, part, own):
            raised = win.at[8, part]
            self.right = (
                transfer(own, win.at[2, part], right),
                transfer(raised, win.at[2, part], right, len(used) - 1),
            )
            self.left = (
                transfer(own, win.at[6, part], left),
                transfer(raised, win.at[6, part], left, len(used) - 1),
            )

        def from_own(self):
            pl.when(x < 3)(self.right[0].start)
            pl.when(x == 0)(self.left[0].start)
            sent.extend((self.right[0], self.left[0]))

        def from_raised(self):
            pl.when(x == 3)(self.right[1].start)
            pl.when(x > 0)(self.left[1].start)

    k_open = ring_open(k_ref, kw, 0)
    v_parts = (rows(0, 0), rows(0, 1))
    v_src = (v_ref.at[pl.ds(0, HALF)], v_ref.at[pl.ds(HALF, HALF)])
    v_up, v_side = [], []
    for src, part in zip(v_src, v_parts):
        v_up.append(climb(src, vw, part))
        v_side.append(Sideways(vw, part, src))
        v_side[-1].from_own()

    def share(win, slot, base):
        def start(index):
            copy = transfer(win.at[slot], win.at[2 * index + 1], sibling, base + index)
            copy.start()

        if slot == 0:
            pl.when(core == 0)(lambda: start(0))
        elif slot == 8:
            pl.when(core == 1)(lambda: start(3))
        else:
            start(slot // 2 - core)

    k_share, v_share = len(used), len(used) + 4
    used.extend(range(len(used), len(used) + 8))

    k_up, k_side = [], []

    def key_chunk(order, src):
        k_up.append(climb(src, kw, rows(order)))
        k_side.append(Sideways(kw, rows(order), src))
        k_side[-1].from_own()

    key_chunk(0, k_ref)
    v0 = ring_open(v_ref, vw, 0)
    keep_k.wait()
    keep_v.wait()

    k_open[0].wait_recv()
    k_pass0 = go(transfer(kw.at[0, rows(3, 0)], kw.at[0, rows(3, 0)], after))
    key_chunk(3, kw.at[0, rows(3)])
    k_open[1].wait_recv()
    k_pass1 = go(transfer(kw.at[0, rows(1, 1)], kw.at[0, rows(1, 1)], before))
    key_chunk(1, kw.at[0, rows(1)])

    for copy, side in zip(v_up, v_side):
        copy.wait_recv()
        side.from_raised()

    k_pass0.wait_recv()
    k_pass1.wait_recv()
    key_chunk(2, kw.at[0, rows(2)])
    share(kw, 0, k_share)

    v_side[0].right[0].wait_recv()
    v_mid0 = go(transfer(vw.at[2, v_parts[0]], vw.at[4, v_parts[0]], follower))
    v_side[1].right[0].wait_recv()
    v2 = ring_open(vw.at[2, rows(0)], vw, 2)
    v_side[1].left[0].wait_recv()
    v_mid1 = go(transfer(vw.at[6, v_parts[1]], vw.at[4, v_parts[1]], leader))
    v_side[0].left[0].wait_recv()

    k_up[0].wait_recv()
    k_side[0].from_raised()
    v0p = ring_pass(vw, 0, v0)
    v6 = ring_open(vw.at[6, rows(0)], vw, 6)
    k_up[1].wait_recv()
    k_side[1].from_raised()

    k_mid = [None] * 4
    orders = (0, 3, 1, 2)

    def relay_right(i):
        k_side[i].right[0].wait_recv()
        part = rows(orders[i])
        k_mid[i] = go(transfer(kw.at[2, part], kw.at[4, part], follower))

    def relay_left(i):
        k_side[i].left[0].wait_recv()
        part = rows(orders[i])
        k_mid[i] = go(transfer(kw.at[6, part], kw.at[4, part], leader))

    relay_right(0)
    v_mid0.wait_recv()
    v_mid1.wait_recv()
    v4 = ring_open(vw.at[4, rows(0)], vw, 4)
    v2p = ring_pass(vw, 2, v2)
    k_up[2].wait_recv()
    k_side[2].from_raised()
    ring_close(v0p)
    share(vw, 0, v_share)
    relay_right(1)
    k_up[3].wait_recv()
    k_side[3].from_raised()
    v6p = ring_pass(vw, 6, v6)

    far = len(used)
    used.extend(range(far, far + 4))
    far_open = (
        transfer(vw.at[8, rows(0)], vw.at[8, rows(0)], after, far),
        transfer(vw.at[8, rows(0)], vw.at[8, rows(0)], before, far + 1),
    )
    far_pass = (
        transfer(vw.at[8, rows(3, 0)], vw.at[8, rows(3, 0)], after, far + 2),
        transfer(vw.at[8, rows(1, 1)], vw.at[8, rows(1, 1)], before, far + 3),
    )

    @pl.when(core == 1)
    def _():
        far_open[0].start()
        far_open[1].start()

    ring_close(v2p)
    share(vw, 2, v_share)
    relay_left(2)
    share(kw, 8, k_share)
    v4p = ring_pass(vw, 4, v4)
    relay_left(3)
    k_side[2].right[0].wait_recv()
    k_side[3].right[0].wait_recv()
    share(kw, 2, k_share)

    @pl.when(core == 1)
    def _():
        far_open[0].wait_recv()
        far_pass[0].start()
        far_open[1].wait_recv()
        far_pass[1].start()

    ring_close(v6p)
    share(vw, 6, v_share)
    k_side[0].left[0].wait_recv()
    k_side[1].left[0].wait_recv()
    share(kw, 6, k_share)
    ring_close(v4p)
    share(vw, 4, v_share)

    @pl.when(core == 1)
    def _():
        far_pass[0].wait_recv()
        far_pass[1].wait_recv()

    share(vw, 8, v_share)
    for copy in k_mid:
        copy.wait_recv()
    share(kw, 4, k_share)

    for base, win in ((k_share, kw), (v_share, vw)):
        for index in range(4):
            copy = transfer(win.at[2 * index + 1], win.at[2 * index + 1], sibling, base + index)
            copy.wait_recv()
            copy.wait_send()
    for copy in sent:
        copy.wait_send()

    @pl.when(core == 1)
    def _():
        for copy in far_open + far_pass:
            copy.wait_send()


def gather_windows(keys, values):
    depth = keys.shape[1]
    window = jax.ShapeDtypeStruct((REACH + 2, BLOCK * SLOTS, depth), keys.dtype)
    count = 96
    return pl.pallas_call(
        gather_kernel,
        out_shape=(window, window),
        in_specs=[pl.BlockSpec(memory_space=pl.ANY)] * 2,
        out_specs=(pl.BlockSpec(memory_space=pl.ANY),) * 2,
        scratch_shapes=[
            pltpu.SemaphoreType.DMA((count,)),
            pltpu.SemaphoreType.DMA((count,)),
            pltpu.SemaphoreType.DMA((2,)),
        ],
        compiler_params=pltpu.CompilerParams(collective_id=0, has_side_effects=True),
        name="gather_windows",
    )(keys, values)


def attend_kernel(
    lengths, counts, q_ref, kw, vw, out_ref, kbuf, vbuf, scores, top, total, first, table, sems
):
    heads = q_ref.shape[1] // 128
    inner = lax.axis_index("inner")
    me = lax.axis_index("outer") * 16 + inner
    count = counts[me]
    before = lax.fori_loop(0, me, lambda i, t: t + counts[i], 0)
    base = before * BLOCK
    docs = lengths.shape[0]

    table[0] = 1
    table[1] = 0
    filled = jnp.int32(2)
    for distance in range(1, REACH + 1):
        source = me - distance
        held = jnp.where(source >= 0, counts[jnp.maximum(source, 0)], 0)
        table[filled] = distance * SLOTS + held - 1
        table[filled + 1] = distance * SLOTS
        filled = filled + held

    def start_of(position):
        def step(i, carry):
            running, best = carry
            best = jnp.where(running <= position, running, best)
            return running + lengths[i], best

        return lax.fori_loop(0, docs, step, (jnp.int32(0), jnp.int32(0)))[1]

    lowest = start_of(base)
    needed = before - lowest // BLOCK + 1

    def fetch(entry, which):
        place = table[entry]
        window, buffer, sem = ((kw, kbuf, 0), (vw, vbuf, 1))[which]
        source = window.at[
            place // SLOTS, pl.ds(pl.multiple_of(lax.rem(place, SLOTS) * BLOCK, BLOCK), BLOCK)
        ]
        return pltpu.make_async_copy(source, buffer.at[entry], sems.at[sem, entry])

    def start_fetch(which):
        def one(i, carry):
            fetch(1 + i, which).start()
            return carry

        lax.fori_loop(0, needed, one, 0)

        @pl.when(count == SLOTS)
        def _():
            fetch(0, which).start()

    start_fetch(0)
    start_fetch(1)

    scale = math.log2(math.e) / math.sqrt(128)
    ones = jnp.ones((BLOCK, 128), jnp.bfloat16)

    def block(slot):
        begin = base + slot * BLOCK
        low = lowest if slot == 0 else start_of(begin)
        high = start_of(begin + BLOCK - 1)
        number = (begin - low // BLOCK * BLOCK) // BLOCK + 1
        position = begin + lax.broadcasted_iota(jnp.int32, (BLOCK, 128), 0)
        first[...] = jnp.full((BLOCK, 128), low, jnp.int32)

        def mark(i, running):
            @pl.when((running > begin) & (running < begin + BLOCK))
            def _():
                first[...] = jnp.where(position >= running, running, first[...])

            return running + lengths[i]

        @pl.when(high != low)
        def _():
            lax.fori_loop(0, docs, mark, jnp.int32(0))

        top[...] = jnp.full(top.shape, NEGATIVE, jnp.float32)
        span = pl.ds(slot * BLOCK, BLOCK)

        def score(j, carry):
            entry = 1 - slot + j
            if slot == 0:
                fetch(entry, 0).wait()
            else:

                @pl.when(j == 0)
                def _():
                    fetch(0, 0).wait()

            key_begin = begin - j * BLOCK
            products = []
            for h in range(heads):
                products.append(
                    lax.dot_general(
                        q_ref[span, h * 128 : (h + 1) * 128],
                        kbuf[entry],
                        (((1,), (1,)), ((), ())),
                        preferred_element_type=jnp.float32,
                    )
                )

            def keep(mask):
                for h in range(heads):
                    best = top[h]
                    for part in range(BLOCK // 128):
                        lanes = slice(part * 128, (part + 1) * 128)
                        piece = products[h][:, lanes]
                        if mask is not None:
                            piece = jnp.where(mask[part], piece, NEGATIVE)
                        scores[j, h, :, lanes] = piece
                        best = jnp.maximum(best, piece)
                    top[h] = best

            plain = (j > 0) & (key_begin >= high)

            @pl.when(plain)
            def _():
                keep(None)

            @pl.when(jnp.logical_not(plain))
            def _():
                masks = []
                for part in range(BLOCK // 128):
                    key = key_begin + part * 128 + lax.broadcasted_iota(jnp.int32, (BLOCK, 128), 1)
                    masks.append((key >= first[...]) & (key <= position))
                keep(masks)

            return carry

        lax.fori_loop(0, number, score, 0)

        for h in range(heads):
            best = jnp.max(top[h], axis=1, keepdims=True) * scale
            top[h] = jnp.broadcast_to(best, (BLOCK, 128))
        total[...] = jnp.zeros(total.shape, jnp.float32)

        def weigh(j, carry):
            entry = 1 - slot + j
            if slot == 0:
                fetch(entry, 1).wait()
            else:

                @pl.when(j == 0)
                def _():
                    fetch(0, 1).wait()

            widened = jnp.concatenate([vbuf[entry], ones], axis=1)
            for h in range(heads):
                weights = []
                for part in range(BLOCK // 128):
                    lanes = slice(part * 128, (part + 1) * 128)
                    weights.append(jnp.exp2(scores[j, h, :, lanes] * scale - top[h]).astype(jnp.bfloat16))
                total[h] += jnp.dot(
                    jnp.concatenate(weights, axis=1), widened, preferred_element_type=jnp.float32
                )
            return carry

        lax.fori_loop(0, number, weigh, 0)
        for h in range(heads):
            result = total[h, :, :128] / total[h, :, 128:]
            out_ref[span, h * 128 : (h + 1) * 128] = result.astype(out_ref.dtype)

    block(0)

    @pl.when(count == SLOTS)
    def _():
        block(1)

    @pl.when(count != SLOTS)
    def _():
        out_ref[BLOCK:, :] = jnp.zeros((BLOCK, out_ref.shape[1]), out_ref.dtype)


def attend(lengths, counts, queries, kw, vw):
    heads = queries.shape[1] // 128
    entries = REACH + 2
    return pl.pallas_call(
        attend_kernel,
        out_shape=jax.ShapeDtypeStruct(queries.shape, jnp.bfloat16),
        in_specs=[
            pl.BlockSpec(memory_space=pltpu.SMEM),
            pl.BlockSpec(memory_space=pltpu.SMEM),
            pl.BlockSpec(memory_space=pltpu.VMEM),
            pl.BlockSpec(memory_space=pl.ANY),
            pl.BlockSpec(memory_space=pl.ANY),
        ],
        out_specs=pl.BlockSpec(memory_space=pltpu.VMEM),
        scratch_shapes=[
            pltpu.VMEM((entries, BLOCK, 128), jnp.bfloat16),
            pltpu.VMEM((entries, BLOCK, 128), jnp.bfloat16),
            pltpu.VMEM((REACH + 1, heads, BLOCK, BLOCK), jnp.float32),
            pltpu.VMEM((heads, BLOCK, 128), jnp.float32),
            pltpu.VMEM((heads, BLOCK, 256), jnp.float32),
            pltpu.VMEM((BLOCK, 128), jnp.int32),
            pltpu.SMEM((2 * REACH + 4,), jnp.int32),
            pltpu.SemaphoreType.DMA((2, entries)),
        ],
        compiler_params=pltpu.CompilerParams(vmem_limit_bytes=48 * 2**20),
        name="attend",
    )(lengths, counts, queries, kw, vw)


def shards(queries, keys, values, doc_lengths, block_count):
    kw, vw = gather_windows(keys, values)
    return attend(doc_lengths, block_count, queries, kw, vw)


def solution(mesh):
    placed = (
        P(("outer", "inner"), "head"),
        P(("outer", "inner", "head"), None),
        P(("outer", "inner", "head"), None),
        P(),
        P(),
    )
    return jax.shard_map(
        shards, mesh=mesh, in_specs=placed, out_specs=P(("outer", "inner"), "head"), check_vma=False
    )
```

```python
import math

import jax
import jax.numpy as jnp
from jax import lax
from jax.experimental import pallas as pl
from jax.experimental.pallas import tpu as pltpu
from jax.sharding import PartitionSpec as P

BLOCK = 512
SLOTS = 2
REACH = 7
QUARTER = 256
HALF = 128
MESH = pl.DeviceIdType.MESH
NEGATIVE = -1e30


def gather_kernel(k_ref, v_ref, kw, vw, send_sems, recv_sems, local_sems):
    outer = lax.axis_index("outer")
    inner = lax.axis_index("inner")
    y = lax.axis_index("head")
    z = outer * 2 + inner // 8
    x = lax.rem(inner // 2, 4)
    core = lax.rem(inner, 2)

    def place(px, py, pz, pc):
        return (pz // 2, lax.rem(pz, 2) * 8 + px * 2 + pc, py)

    xp, xm = lax.rem(x + 1, 4), lax.rem(x + 3, 4)
    yp, ym = lax.rem(y + 1, 4), lax.rem(y + 3, 4)
    zp, zm = lax.rem(z + 1, 8), lax.rem(z + 7, 8)
    z_next = jnp.where(x == 3, zp, z)
    z_prev = jnp.where(x == 0, zm, z)
    right, left = place(xp, y, z, core), place(xm, y, z, core)
    up, down = place(x, y, zp, core), place(x, y, zm, core)
    after, before = place(x, yp, z, core), place(x, ym, z, core)
    follower, leader = place(xp, y, z_next, core), place(xm, y, z_prev, core)
    sibling = place(x, y, z, 1 - core)

    barrier = pltpu.get_barrier_semaphore()
    for partner in (right, left, up, down, after, before, follower, leader, sibling):
        pl.semaphore_signal(barrier, inc=1, device_id=partner, device_id_type=MESH)

    def rows(order, half=None):
        start = lax.rem(y + order, 4) * QUARTER
        if half is None:
            return pl.ds(pl.multiple_of(start, QUARTER), QUARTER)
        return pl.ds(pl.multiple_of(start + half * HALF, HALF), HALF)

    sems, arrived, sent = {}, set(), []

    def transfer(name, src, dst, device):
        sem = sems.setdefault(name, len(sems))
        return pltpu.make_async_remote_copy(
            src_ref=src,
            dst_ref=dst,
            send_sem=send_sems.at[sem],
            recv_sem=recv_sems.at[sem],
            device_id=device,
            device_id_type=MESH,
        )

    shapes = {}

    def post(name, src, dst, device, when=None, track=True):
        copy = transfer(name, src, dst, device)
        if when is None:
            copy.start()
        else:
            pl.when(when)(copy.start)
        shapes[name] = dst
        if track:
            sent.append(name)

    def finish(name, dst):
        return transfer(name, dst, dst, sibling)

    def need(*names):
        for name in names:
            if name not in arrived:
                arrived.add(name)
                finish(name, places[name]).wait_recv()

    places = {}
    for order in range(4):
        part = rows(order)
        places["ku", order] = kw.at[8, part]
        places["kr", order] = kw.at[2, part]
        places["kl", order] = kw.at[6, part]
        places["km", order] = kw.at[4, part]
    for half in range(2):
        part = rows(0, half)
        places["vu", half] = vw.at[8, part]
        places["vr", half] = vw.at[2, part]
        places["vl", half] = vw.at[6, part]
        places["vm", half] = vw.at[4, part]
    for win, ring, slots in ((kw, "k", (0,)), (vw, "v", (0, 2, 4, 6, 8))):
        for slot in slots:
            places[ring, slot, 0] = win.at[slot, rows(3)]
            places[ring, slot, 1] = win.at[slot, rows(1)]
            places[ring, slot, 2] = win.at[slot, rows(2, 0)]
            places[ring, slot, 3] = win.at[slot, rows(2, 1)]

    keep_k = pltpu.make_async_copy(k_ref, kw.at[0, rows(0)], local_sems.at[0])
    keep_v = pltpu.make_async_copy(v_ref, vw.at[0, rows(0)], local_sems.at[1])
    keep_k.start()
    keep_v.start()
    pl.semaphore_wait(barrier, 9)

    def key_open():
        post(("k", 0, 0), k_ref, kw.at[0, rows(0)], after)
        post(("k", 0, 1), k_ref, kw.at[0, rows(0)], before)

    def key_pass(side):
        need(("k", 0, side))
        part = rows((3, 1)[side], side)
        post(("k", 0, 2 + side), kw.at[0, part], kw.at[0, part], (after, before)[side])

    def send(kind, win, index, part, own):
        post((kind + "u", index), own, win.at[8, part], up)
        post((kind + "r", index), own, win.at[2, part], right, x < 3)
        post((kind + "l", index), own, win.at[6, part], left, x == 0)

    def turn(kind, win, index, part):
        need((kind + "u", index))
        post((kind + "r", index), win.at[8, part], win.at[2, part], right, x == 3, False)
        post((kind + "l", index), win.at[8, part], win.at[6, part], left, x > 0, False)

    def relay(kind, win, index, part, forward):
        slot, source = (2, "r") if forward else (6, "l")
        need((kind + source, index))
        post((kind + "m", index), win.at[slot, part], win.at[4, part], follower if forward else leader)

    def key_send(order):
        if order == 3:
            need(("k", 0, 0))
        if order == 1:
            need(("k", 0, 1))
        if order == 2:
            need(("k", 0, 2), ("k", 0, 3))
        send("k", kw, order, rows(order), k_ref if order == 0 else kw.at[0, rows(order)])

    def key_turn(order):
        turn("k", kw, order, rows(order))

    def key_relay(order):
        relay("k", kw, order, rows(order), order in (0, 3))

    def value_send(half):
        send("v", vw, half, rows(0, half), v_ref.at[pl.ds(half * HALF, HALF)])

    def value_turn(half):
        turn("v", vw, half, rows(0, half))

    def value_relay(half):
        relay("v", vw, half, rows(0, half), half == 0)

    def only(slot, run):
        if slot == 8:
            pl.when(core == 1)(run)
        else:
            run()

    def ring_open(slot):
        if slot:
            source = {2: "vr", 4: "vm", 6: "vl", 8: "vu"}[slot]
            need((source, 0), (source, 1))
        own = vw.at[slot, rows(0)]

        def run():
            post(("v", slot, 0), own if slot else v_ref, own, after, track=slot != 8)
            post(("v", slot, 1), own if slot else v_ref, own, before, track=slot != 8)

        only(slot, run)

    def ring_pass(slot):
        parts = [vw.at[slot, rows(3, 0)], vw.at[slot, rows(1, 1)]]

        def run():
            for side, part in enumerate(parts):
                need(("v", slot, side))
                post(
                    ("v", slot, 2 + side),
                    part,
                    part,
                    (after, before)[side],
                    track=slot != 8,
                )

        only(slot, run)

    kept = []

    def keep():
        if not kept:
            kept.append(True)
            keep_k.wait()
            keep_v.wait()

    def share(win, slot):
        kind = "k" if win is kw else "v"
        if slot == 0:
            keep()
        if kind == "k" and slot:
            source = {2: "kr", 6: "kl", 8: "ku"}[slot]
            need(*((source, order) for order in range(4)))
        elif kind == "k":
            need(*(("k", 0, i) for i in range(4)))

        there = win.at[slot + 1 - 2 * core]

        def run():
            if kind == "v":
                need(*(("v", slot, i) for i in range(4)))
            if slot == 0:
                post((kind + "c", slot), win.at[slot], there, sibling, core == 0, False)
            else:
                post((kind + "c", slot), win.at[slot], there, sibling, track=slot != 8)

        only(slot, run)

    def share_middle_keys(order):
        need(("km", order))
        part = rows(order)
        post(("kc", 4, order), kw.at[4, part], kw.at[5 - 2 * core, part], sibling)

    def share_middle_values(step):
        if step == 0:
            need(("vm", 0), ("vm", 1), ("v", 4, 0), ("v", 4, 1))
            parts = (0, 3, 1)
        else:
            need(("v", 4, 2), ("v", 4, 3))
            parts = (2,)
        for order in parts:
            part = rows(order)
            post(("vc", 4, order), vw.at[4, part], vw.at[5 - 2 * core, part], sibling)

    value_send(0)
    value_send(1)
    key_open()
    key_send(0)
    key_send(1)
    ring_open(0)
    value_turn(0)
    key_send(3)
    ring_open(8)
    value_turn(1)
    key_turn(0)
    key_pass(1)
    value_relay(0)
    key_pass(0)
    value_relay(1)
    ring_pass(0)
    key_turn(1)
    ring_pass(8)
    ring_open(2)
    key_send(2)
    ring_open(6)
    key_turn(3)
    key_turn(2)
    key_relay(0)
    share(vw, 0)
    ring_open(4)
    share(kw, 8)
    key_relay(1)
    share(vw, 8)
    ring_pass(6)
    key_relay(3)
    share(kw, 6)
    ring_pass(2)
    key_relay(2)
    ring_pass(4)
    share(kw, 0)
    share_middle_keys(1)
    share(kw, 2)
    share(vw, 6)
    share_middle_values(0)
    share_middle_keys(0)
    share(vw, 2)
    share_middle_keys(3)
    share_middle_values(1)
    share_middle_keys(2)
    keep()
    for kind, win in (("k", kw), ("v", vw)):
        for order in range(4):
            finish((kind + "c", 4, order), win.at[5, rows(order)]).wait_recv()
        for slot in (2, 6):
            finish((kind + "c", slot), win.at[slot]).wait_recv()

        @pl.when(core == 1)
        def _(kind=kind, win=win):
            finish((kind + "c", 0), win.at[0]).wait_recv()
            finish((kind + "c", 8), win.at[8]).wait_send()

        @pl.when(core == 0)
        def _(kind=kind, win=win):
            finish((kind + "c", 0), win.at[0]).wait_send()
            finish((kind + "c", 8), win.at[8]).wait_recv()

    @pl.when(core == 1)
    def _():
        for i in range(4):
            finish(("v", 8, i), shapes["v", 8, i]).wait_send()

    for name in sent:
        finish(name, shapes[name]).wait_send()


def gather_windows(keys, values):
    depth = keys.shape[1]
    window = jax.ShapeDtypeStruct((REACH + 2, BLOCK * SLOTS, depth), keys.dtype)
    count = 96
    return pl.pallas_call(
        gather_kernel,
        out_shape=(window, window),
        in_specs=[pl.BlockSpec(memory_space=pl.ANY)] * 2,
        out_specs=(pl.BlockSpec(memory_space=pl.ANY),) * 2,
        scratch_shapes=[
            pltpu.SemaphoreType.DMA((count,)),
            pltpu.SemaphoreType.DMA((count,)),
            pltpu.SemaphoreType.DMA((2,)),
        ],
        compiler_params=pltpu.CompilerParams(collective_id=0, has_side_effects=True),
        name="gather_windows",
    )(keys, values)


def attend_kernel(
    lengths, counts, q_hbm, kw, vw, out_hbm, qbuf, kbuf, vbuf, scores, top, total, first, obuf, table, sems, io_sems
):
    heads = q_hbm.shape[1] // 128
    contexts = counts.shape[0]
    docs = lengths.shape[0]
    spans = [pl.ds(slot * BLOCK, BLOCK) for slot in range(SLOTS)]
    q_in = [
        pltpu.make_async_copy(
            q_hbm.at[spans[slot], h * 128 : (h + 1) * 128],
            qbuf.at[slot, pl.ds(h * BLOCK, BLOCK)],
            io_sems.at[0, slot * heads + h],
        )
        for slot in range(SLOTS)
        for h in range(heads)
    ]
    outs = [pltpu.make_async_copy(obuf.at[s], out_hbm.at[s], io_sems.at[1, i]) for i, s in enumerate(spans)]
    for copy in q_in:
        copy.start()

    me = lax.axis_index("outer") * 16 + lax.axis_index("inner")
    count = counts[me]
    before = jnp.int32(0)
    for i in range(contexts):
        before = before + jnp.where(i < me, counts[i], 0)
    base = before * BLOCK
    ends = []
    running = jnp.int32(0)
    for i in range(docs):
        running = running + lengths[i]
        ends.append(running)

    def start_of(position):
        best = jnp.int32(0)
        for end in ends:
            best = jnp.where(end <= position, end, best)
        return best

    table[0] = 1
    table[1] = 0
    filled = jnp.int32(2)
    for distance in range(1, REACH + 1):
        source = me - distance
        held = jnp.where(source >= 0, counts[jnp.maximum(source, 0)], 0)
        table[filled] = distance * SLOTS + held - 1
        table[filled + 1] = distance * SLOTS
        filled = filled + held

    lowest = start_of(base)
    needed = before - lowest // BLOCK + 1

    def fetch(entry, which):
        place = table[entry]
        window, buffer, sem = ((kw, kbuf, 0), (vw, vbuf, 1))[which]
        source = window.at[
            place // SLOTS, pl.ds(pl.multiple_of(lax.rem(place, SLOTS) * BLOCK, BLOCK), BLOCK)
        ]
        return pltpu.make_async_copy(source, buffer.at[entry], sems.at[sem, entry])

    for which in range(2):

        def one(i, carry):
            fetch(1 + i, which).start()
            return carry

        lax.fori_loop(0, needed, one, 0)

        @pl.when(count == SLOTS)
        def _():
            fetch(0, which).start()

    scale = math.log2(math.e) / math.sqrt(128)

    def block(slot):
        begin = base + slot * BLOCK
        low = lowest if slot == 0 else start_of(begin)
        high = start_of(begin + BLOCK - 1)
        number = (begin - low // BLOCK * BLOCK) // BLOCK + 1
        plain_end = jnp.maximum((begin - high) // BLOCK, 0) + 1
        position = begin + lax.broadcasted_iota(jnp.int32, (BLOCK, 128), 0)
        first[...] = jnp.full((BLOCK, 128), low, jnp.int32)

        def mark(i, running):
            @pl.when((running > begin) & (running < begin + BLOCK))
            def _():
                first[...] = jnp.where(position >= running, running, first[...])

            return running + lengths[i]

        @pl.when(high != low)
        def _():
            lax.fori_loop(0, docs, mark, jnp.int32(0))

        for h in range(heads):
            q_in[slot * heads + h].wait()

        def wait_for(j, width, which):
            if slot == 0:
                for step in range(width):
                    fetch(1 + j + step, which).wait()
            elif isinstance(j, int) and j == 0:
                fetch(0, which).wait()

        def score(j, width, masked, fresh):
            entry = 1 - slot + j
            wait_for(j, width, 0)
            product = lax.dot_general(
                qbuf[slot],
                kbuf[pl.ds(entry, width)].reshape(width * BLOCK, 128),
                (((1,), (1,)), ((), ())),
                preferred_element_type=jnp.float32,
            )
            best = [None if fresh else top[h] for h in range(heads)]
            for step in range(width):
                for part in range(BLOCK // 128):
                    if masked:
                        key = (
                            begin
                            - (j + step) * BLOCK
                            + part * 128
                            + lax.broadcasted_iota(jnp.int32, (BLOCK, 128), 1)
                        )
                        mask = (key >= first[...]) & (key <= position)
                    for h in range(heads):
                        rows = slice(h * BLOCK, (h + 1) * BLOCK)
                        piece = product[rows, step * BLOCK + part * 128 : step * BLOCK + (part + 1) * 128]
                        if masked:
                            piece = jnp.where(mask, piece, NEGATIVE)
                        scores[j + step, rows, part * 128 : (part + 1) * 128] = piece
                        best[h] = piece if best[h] is None else jnp.maximum(best[h], piece)
            for h in range(heads):
                top[h] = best[h]

        def weigh(j, width, fresh):
            entry = 1 - slot + j
            wait_for(j, width, 1)
            value = vbuf[pl.ds(entry, width)].reshape(width * BLOCK, 128)
            widened = jnp.concatenate([value, jnp.ones_like(value)], axis=1)
            highest = top[...].reshape(heads * BLOCK, 128)
            weights = []
            for step in range(width):
                for part in range(BLOCK // 128):
                    shifted = scores[j + step, :, part * 128 : (part + 1) * 128] * scale - highest
                    weights.append(jnp.exp2(shifted).astype(jnp.bfloat16))
            product = jnp.dot(
                jnp.concatenate(weights, axis=1), widened, preferred_element_type=jnp.float32
            )
            if fresh:
                total[...] = product
            else:
                total[...] += product

        pairs = number // 2
        plain_pairs = jnp.clip(plain_end // 2, 1, jnp.maximum(pairs, 1))
        alone = number == 1
        odd = (number > 1) & (lax.rem(number, 2) == 1)

        def looped(body):
            def step(i, carry):
                body(2 * i)
                return carry

            return step

        @pl.when(alone)
        def _():
            score(0, 1, True, True)

        @pl.when(jnp.logical_not(alone))
        def _():
            score(0, 2, True, True)

        lax.fori_loop(1, plain_pairs, looped(lambda j: score(j, 2, False, False)), 0)
        lax.fori_loop(plain_pairs, pairs, looped(lambda j: score(j, 2, True, False)), 0)

        @pl.when(odd)
        def _():
            score(number - 1, 1, True, False)

        for h in range(heads):
            best = jnp.max(top[h], axis=1, keepdims=True) * scale
            top[h] = jnp.broadcast_to(best, (BLOCK, 128))

        @pl.when(alone)
        def _():
            weigh(0, 1, True)

        @pl.when(jnp.logical_not(alone))
        def _():
            weigh(0, 2, True)

        lax.fori_loop(1, pairs, looped(lambda j: weigh(j, 2, False)), 0)

        @pl.when(odd)
        def _():
            weigh(number - 1, 1, False)

        for h in range(heads):
            rows = slice(h * BLOCK, (h + 1) * BLOCK)
            result = total[rows, :128] / total[rows, 128:]
            obuf[spans[slot], h * 128 : (h + 1) * 128] = result.astype(obuf.dtype)
        outs[slot].start()

    block(0)

    @pl.when(count == SLOTS)
    def _():
        block(1)

    @pl.when(count != SLOTS)
    def _():
        obuf[spans[1], :] = jnp.zeros((BLOCK, obuf.shape[1]), obuf.dtype)
        for h in range(heads):
            q_in[heads + h].wait()
        outs[1].start()

    for copy in outs:
        copy.wait()


def attend(lengths, counts, queries, kw, vw):
    heads = queries.shape[1] // 128
    entries = REACH + 2
    return pl.pallas_call(
        attend_kernel,
        out_shape=jax.ShapeDtypeStruct(queries.shape, jnp.bfloat16),
        in_specs=[
            pl.BlockSpec(memory_space=pltpu.SMEM),
            pl.BlockSpec(memory_space=pltpu.SMEM),
            pl.BlockSpec(memory_space=pl.ANY),
            pl.BlockSpec(memory_space=pl.ANY),
            pl.BlockSpec(memory_space=pl.ANY),
        ],
        out_specs=pl.BlockSpec(memory_space=pl.ANY),
        scratch_shapes=[
            pltpu.VMEM((SLOTS, heads * BLOCK, 128), jnp.bfloat16),
            pltpu.VMEM((entries, BLOCK, 128), jnp.bfloat16),
            pltpu.VMEM((entries, BLOCK, 128), jnp.bfloat16),
            pltpu.VMEM((REACH + 1, heads * BLOCK, BLOCK), jnp.float32),
            pltpu.VMEM((heads, BLOCK, 128), jnp.float32),
            pltpu.VMEM((heads * BLOCK, 256), jnp.float32),
            pltpu.VMEM((BLOCK, 128), jnp.int32),
            pltpu.VMEM(queries.shape, jnp.bfloat16),
            pltpu.SMEM((2 * REACH + 4,), jnp.int32),
            pltpu.SemaphoreType.DMA((2, entries)),
            pltpu.SemaphoreType.DMA((2, SLOTS * heads)),
        ],
        compiler_params=pltpu.CompilerParams(vmem_limit_bytes=60 * 2**20),
        name="attend",
    )(lengths, counts, queries, kw, vw)


def shards(queries, keys, values, doc_lengths, block_count):
    kw, vw = gather_windows(keys, values)
    return attend(doc_lengths, block_count, queries, kw, vw)


def solution(mesh):
    placed = (
        P(("outer", "inner"), "head"),
        P(("outer", "inner", "head"), None),
        P(("outer", "inner", "head"), None),
        P(),
        P(),
    )
    return jax.shard_map(
        shards, mesh=mesh, in_specs=placed, out_specs=P(("outer", "inner"), "head"), check_vma=False
    )
```

```python
import math

import jax
import jax.numpy as jnp
from jax import lax
from jax.experimental import pallas as pl
from jax.experimental.pallas import tpu as pltpu
from jax.sharding import PartitionSpec as P

BLOCK = 512
SLOTS = 2
REACH = 7
QUARTER = 256
LAYERS = 8
HALF = 128
MESH = pl.DeviceIdType.MESH
NEGATIVE = -1e30


def gather_kernel(k_ref, v_ref, kw, vw, send_sems, recv_sems, local_sems):
    outer = lax.axis_index("outer")
    inner = lax.axis_index("inner")
    y = lax.axis_index("head")
    z = outer * 2 + inner // 8
    x = lax.rem(inner // 2, 4)
    core = lax.rem(inner, 2)

    def place(px, py, pz, pc):
        return (pz // 2, lax.rem(pz, 2) * 8 + px * 2 + pc, py)

    xp, xm = lax.rem(x + 1, 4), lax.rem(x + 3, 4)
    yp, ym = lax.rem(y + 1, 4), lax.rem(y + 3, 4)
    zp, zm = lax.rem(z + 1, LAYERS), lax.rem(z + LAYERS - 1, LAYERS)
    z_next = jnp.where(x == 3, zp, z)
    z_prev = jnp.where(x == 0, zm, z)
    right, left = place(xp, y, z, core), place(xm, y, z, core)
    up, down = place(x, y, zp, core), place(x, y, zm, core)
    after, before = place(x, yp, z, core), place(x, ym, z, core)
    follower, leader = place(xp, y, z_next, core), place(xm, y, z_prev, core)
    sibling = place(x, y, z, 1 - core)

    chip = z * 4 + x
    last = LAYERS * 4 - 1
    has_up, has_down = z < LAYERS - 1, z > 0
    barrier = pltpu.get_barrier_semaphore()

    def greet(partner):
        pl.semaphore_signal(barrier, inc=1, device_id=partner, device_id_type=MESH)

    for partner in (right, left, after, before, sibling):
        greet(partner)
    pl.when(has_up)(lambda: greet(up))
    pl.when(has_down)(lambda: greet(down))
    pl.when(chip < last)(lambda: greet(follower))
    pl.when(chip > 0)(lambda: greet(leader))

    def one(flag):
        return jnp.where(flag, 1, 0)

    partners = 5 + one(has_up) + one(has_down) + one(chip < last) + one(chip > 0)

    def present(name):
        if name[0] in ("k", "v"):
            return None if name[1] == 0 else chip >= name[1] // 2
        return chip >= {"u": 4, "r": 1, "l": 3, "m": 2}[name[0][1]]

    def under(flag, run):
        if flag is None:
            run()
        else:
            pl.when(flag)(run)

    def rows(order, half=None):
        start = lax.rem(y + order, 4) * QUARTER
        if half is None:
            return pl.ds(pl.multiple_of(start, QUARTER), QUARTER)
        return pl.ds(pl.multiple_of(start + half * HALF, HALF), HALF)

    sems, arrived, sent = {}, set(), []

    def transfer(name, src, dst, device, arrives=None):
        sem = sems.setdefault(name, len(sems))
        end = sems.setdefault(arrives or name, len(sems))
        return pltpu.make_async_remote_copy(
            src_ref=src,
            dst_ref=dst,
            send_sem=send_sems.at[sem],
            recv_sem=recv_sems.at[end],
            device_id=device,
            device_id_type=MESH,
        )

    shapes = {}

    def post(name, src, dst, device, when=None, done=None, arrives=None, track=True):
        under(when, transfer(name, src, dst, device, arrives).start)
        shapes[name] = dst
        if track:
            sent.append((name, when if done is None else done))

    def finish(name, dst):
        return transfer(name, dst, dst, sibling)

    def need(*names):
        for name in names:
            if name not in arrived:
                arrived.add(name)
                under(present(name), finish(name, places[name]).wait_recv)

    places = {}
    for order in range(4):
        part = rows(order)
        places["ku", order] = kw.at[8, part]
        places["kr", order] = kw.at[2, part]
        places["kl", order] = kw.at[6, part]
        places["km", order] = kw.at[4, part]
    for half in range(2):
        part = rows(0, half)
        places["vu", half] = vw.at[8, part]
        places["vr", half] = vw.at[2, part]
        places["vl", half] = vw.at[6, part]
        places["vm", half] = vw.at[4, part]
    for win, ring, slots in ((kw, "k", (0,)), (vw, "v", (0, 2, 4, 6, 8))):
        for slot in slots:
            places[ring, slot, 0] = win.at[slot, rows(3)]
            places[ring, slot, 1] = win.at[slot, rows(1)]
            places[ring, slot, 2] = win.at[slot, rows(2, 0)]
            places[ring, slot, 3] = win.at[slot, rows(2, 1)]

    keep_k = pltpu.make_async_copy(k_ref, kw.at[0, rows(0)], local_sems.at[0])
    keep_v = pltpu.make_async_copy(v_ref, vw.at[0, rows(0)], local_sems.at[1])
    keep_k.start()
    keep_v.start()
    pl.semaphore_wait(barrier, partners)

    def key_open():
        post(("k", 0, 0), k_ref, kw.at[0, rows(0)], after)
        post(("k", 0, 1), k_ref, kw.at[0, rows(0)], before)

    def key_pass(side):
        need(("k", 0, side))
        part = rows((3, 1)[side], side)
        post(("k", 0, 2 + side), kw.at[0, part], kw.at[0, part], (after, before)[side])

    def send(kind, win, index, part, own):
        post((kind + "u", index), own, win.at[8, part], up, has_up)
        post((kind + "r", index), own, win.at[2, part], right, x < 3, (x < 3) | has_down)
        post((kind + "l", index), own, win.at[6, part], left, x == 0, (x == 0) | has_down)

    def turn(kind, win, index, part):
        need((kind + "u", index))
        post((kind + "r", index), win.at[8, part], win.at[2, part], right, (x == 3) & has_down, track=False)
        post((kind + "l", index), win.at[8, part], win.at[6, part], left, (x > 0) & has_down, track=False)

    def relay(kind, win, index, part, forward):
        name, there = (kind + "m", index), win.at[4, part]
        if forward:
            need((kind + "r", index))
            post(name, win.at[2, part], there, follower, (chip > 0) & (chip < last))
        else:
            need((kind + "l", index))
            post(name, win.at[6, part], there, leader, chip >= 3)
            need((kind + "r", index))
            post((kind + "x", index), win.at[2, part], there, follower, chip == last - 1, arrives=name)

    def key_send(order):
        if order == 3:
            need(("k", 0, 0))
        if order == 1:
            need(("k", 0, 1))
        if order == 2:
            need(("k", 0, 2), ("k", 0, 3))
        send("k", kw, order, rows(order), k_ref if order == 0 else kw.at[0, rows(order)])

    def key_turn(order):
        turn("k", kw, order, rows(order))

    def key_relay(order):
        relay("k", kw, order, rows(order), order in (0, 3))

    def value_send(half):
        send("v", vw, half, rows(0, half), v_ref.at[pl.ds(half * HALF, HALF)])

    def value_turn(half):
        turn("v", vw, half, rows(0, half))

    def value_relay(half):
        relay("v", vw, half, rows(0, half), half == 0)

    def only(slot, run):
        if slot == 8:
            pl.when((core == 1) & (chip >= 4))(run)
        elif slot:
            pl.when(chip >= slot // 2)(run)
        else:
            run()

    rings = []

    def ring_open(slot):
        if slot:
            source = {2: "vr", 4: "vm", 6: "vl", 8: "vu"}[slot]
            need((source, 0), (source, 1))
        own = vw.at[slot, rows(0)]

        def run():
            post(("v", slot, 0), own if slot else v_ref, own, after, track=False)
            post(("v", slot, 1), own if slot else v_ref, own, before, track=False)

        only(slot, run)
        rings.append(slot)

    def ring_pass(slot):
        parts = [vw.at[slot, rows(3, 0)], vw.at[slot, rows(1, 1)]]

        def run():
            for side, part in enumerate(parts):
                need(("v", slot, side))
                post(
                    ("v", slot, 2 + side),
                    part,
                    part,
                    (after, before)[side],
                    track=False,
                )

        only(slot, run)

    kept = []

    def keep():
        if not kept:
            kept.append(True)
            keep_k.wait()
            keep_v.wait()

    def share(win, slot):
        kind = "k" if win is kw else "v"
        if slot == 0:
            keep()
        if kind == "k" and slot:
            source = {2: "kr", 6: "kl", 8: "ku"}[slot]
            need(*((source, order) for order in range(4)))
        elif kind == "k":
            need(*(("k", 0, i) for i in range(4)))

        there = win.at[slot + 1 - 2 * core]
        if kind == "v":
            only(slot, lambda: need(*(("v", slot, i) for i in range(4))))
        name = (kind + "c", slot)
        if slot == 0:
            post(name, win.at[slot], there, sibling, core == 0)
        elif slot == 8:
            post(name, win.at[slot], there, sibling, core == 1)
        else:
            post(name, win.at[slot], there, sibling)

    def share_middle_keys(order):
        need(("km", order))
        part = rows(order)
        post(("kc", 4, order), kw.at[4, part], kw.at[5 - 2 * core, part], sibling)

    def share_middle_values(step):
        if step == 0:
            need(("vm", 0), ("vm", 1), ("v", 4, 0), ("v", 4, 1))
            parts = (0, 3, 1)
        else:
            need(("v", 4, 2), ("v", 4, 3))
            parts = (2,)
        for order in parts:
            part = rows(order)
            post(("vc", 4, order), vw.at[4, part], vw.at[5 - 2 * core, part], sibling)

    value_send(0)
    value_send(1)
    key_open()
    key_send(0)
    key_send(1)
    ring_open(0)
    value_turn(0)
    key_send(3)
    ring_open(8)
    value_turn(1)
    key_turn(0)
    key_pass(1)
    value_relay(0)
    key_pass(0)
    value_relay(1)
    ring_pass(0)
    key_turn(1)
    ring_pass(8)
    ring_open(2)
    key_send(2)
    ring_open(6)
    key_turn(3)
    key_turn(2)
    key_relay(0)
    share(vw, 0)
    ring_open(4)
    share(kw, 8)
    key_relay(1)
    share(vw, 8)
    ring_pass(6)
    key_relay(3)
    share(kw, 6)
    ring_pass(2)
    key_relay(2)
    ring_pass(4)
    share(kw, 0)
    share_middle_keys(1)
    share(kw, 2)
    share(vw, 6)
    share_middle_values(0)
    share_middle_keys(0)
    share(vw, 2)
    share_middle_keys(3)
    share_middle_values(1)
    share_middle_keys(2)
    keep()
    for kind, win in (("k", kw), ("v", vw)):
        for order in range(4):
            finish((kind + "c", 4, order), win.at[5, rows(order)]).wait_recv()
        for slot in (2, 6):
            finish((kind + "c", slot), win.at[slot]).wait_recv()
        pl.when(core == 1)(finish((kind + "c", 0), win.at[0]).wait_recv)
        pl.when(core == 0)(finish((kind + "c", 8), win.at[8]).wait_recv)

    for name, when in sent:
        under(when, finish(name, shapes[name]).wait_send)
    for slot in rings:

        def close(slot=slot):
            for i in range(4):
                finish(("v", slot, i), shapes["v", slot, i]).wait_send()

        only(slot, close)


def gather_windows(keys, values):
    depth = keys.shape[1]
    window = jax.ShapeDtypeStruct((REACH + 2, BLOCK * SLOTS, depth), keys.dtype)
    count = 112
    return pl.pallas_call(
        gather_kernel,
        out_shape=(window, window),
        in_specs=[pl.BlockSpec(memory_space=pl.ANY)] * 2,
        out_specs=(pl.BlockSpec(memory_space=pl.ANY),) * 2,
        scratch_shapes=[
            pltpu.SemaphoreType.DMA((count,)),
            pltpu.SemaphoreType.DMA((count,)),
            pltpu.SemaphoreType.DMA((2,)),
        ],
        compiler_params=pltpu.CompilerParams(collective_id=0, has_side_effects=True),
        name="gather_windows",
    )(keys, values)


def attend_kernel(
    lengths, counts, q_hbm, kw, vw, out_hbm, qbuf, kbuf, vbuf, scores, top, total, first, obuf, table, sems, io_sems
):
    heads = q_hbm.shape[1] // 128
    contexts = counts.shape[0]
    docs = lengths.shape[0]
    spans = [pl.ds(slot * BLOCK, BLOCK) for slot in range(SLOTS)]
    q_in = [
        pltpu.make_async_copy(
            q_hbm.at[spans[slot], h * 128 : (h + 1) * 128],
            qbuf.at[slot, pl.ds(h * BLOCK, BLOCK)],
            io_sems.at[0, slot * heads + h],
        )
        for slot in range(SLOTS)
        for h in range(heads)
    ]
    outs = [pltpu.make_async_copy(obuf.at[s], out_hbm.at[s], io_sems.at[1, i]) for i, s in enumerate(spans)]
    for copy in q_in:
        copy.start()

    me = lax.axis_index("outer") * 16 + lax.axis_index("inner")
    count = counts[me]
    before = jnp.int32(0)
    for i in range(contexts):
        before = before + jnp.where(i < me, counts[i], 0)
    base = before * BLOCK
    ends = []
    running = jnp.int32(0)
    for i in range(docs):
        running = running + lengths[i]
        ends.append(running)

    def start_of(position):
        best = jnp.int32(0)
        for end in ends:
            best = jnp.where(end <= position, end, best)
        return best

    table[0] = 1
    table[1] = 0
    filled = jnp.int32(2)
    for distance in range(1, REACH + 1):
        source = me - distance
        held = jnp.where(source >= 0, counts[jnp.maximum(source, 0)], 0)
        table[filled] = distance * SLOTS + held - 1
        table[filled + 1] = distance * SLOTS
        filled = filled + held

    lowest = start_of(base)
    needed = before - lowest // BLOCK + 1

    def fetch(entry, which):
        place = table[entry]
        window, buffer, sem = ((kw, kbuf, 0), (vw, vbuf, 1))[which]
        source = window.at[
            place // SLOTS, pl.ds(pl.multiple_of(lax.rem(place, SLOTS) * BLOCK, BLOCK), BLOCK)
        ]
        return pltpu.make_async_copy(source, buffer.at[entry], sems.at[sem, entry])

    for which in range(2):

        def one(i, carry):
            fetch(1 + i, which).start()
            return carry

        lax.fori_loop(0, needed, one, 0)

        @pl.when(count == SLOTS)
        def _():
            fetch(0, which).start()

    scale = math.log2(math.e) / math.sqrt(128)

    def block(slot):
        begin = base + slot * BLOCK
        low = lowest if slot == 0 else start_of(begin)
        high = start_of(begin + BLOCK - 1)
        number = (begin - low // BLOCK * BLOCK) // BLOCK + 1
        plain_end = jnp.maximum((begin - high) // BLOCK, 0) + 1
        position = begin + lax.broadcasted_iota(jnp.int32, (BLOCK, 128), 0)
        first[...] = jnp.full((BLOCK, 128), low, jnp.int32)

        def mark(i, running):
            @pl.when((running > begin) & (running < begin + BLOCK))
            def _():
                first[...] = jnp.where(position >= running, running, first[...])

            return running + lengths[i]

        @pl.when(high != low)
        def _():
            lax.fori_loop(0, docs, mark, jnp.int32(0))

        for h in range(heads):
            q_in[slot * heads + h].wait()

        def wait_for(j, width, which):
            if slot == 0:
                for step in range(width):
                    fetch(1 + j + step, which).wait()
            elif isinstance(j, int) and j == 0:
                fetch(0, which).wait()

        def score(j, width, masked, fresh):
            entry = 1 - slot + j
            wait_for(j, width, 0)
            product = lax.dot_general(
                qbuf[slot],
                kbuf[pl.ds(entry, width)].reshape(width * BLOCK, 128),
                (((1,), (1,)), ((), ())),
                preferred_element_type=jnp.float32,
            )
            best = [None if fresh else top[h] for h in range(heads)]
            for step in range(width):
                for part in range(BLOCK // 128):
                    if masked:
                        key = (
                            begin
                            - (j + step) * BLOCK
                            + part * 128
                            + lax.broadcasted_iota(jnp.int32, (BLOCK, 128), 1)
                        )
                        mask = (key >= first[...]) & (key <= position)
                    for h in range(heads):
                        rows = slice(h * BLOCK, (h + 1) * BLOCK)
                        piece = product[rows, step * BLOCK + part * 128 : step * BLOCK + (part + 1) * 128]
                        if masked:
                            piece = jnp.where(mask, piece, NEGATIVE)
                        scores[j + step, rows, part * 128 : (part + 1) * 128] = piece
                        best[h] = piece if best[h] is None else jnp.maximum(best[h], piece)
            for h in range(heads):
                top[h] = best[h]

        def weigh(j, width, fresh):
            entry = 1 - slot + j
            wait_for(j, width, 1)
            value = vbuf[pl.ds(entry, width)].reshape(width * BLOCK, 128)
            widened = jnp.concatenate([value, jnp.ones_like(value)], axis=1)
            highest = top[...].reshape(heads * BLOCK, 128)
            weights = []
            for step in range(width):
                for part in range(BLOCK // 128):
                    shifted = scores[j + step, :, part * 128 : (part + 1) * 128] * scale - highest
                    weights.append(jnp.exp2(shifted).astype(jnp.bfloat16))
            product = jnp.dot(
                jnp.concatenate(weights, axis=1), widened, preferred_element_type=jnp.float32
            )
            if fresh:
                total[...] = product
            else:
                total[...] += product

        pairs = number // 2
        plain_pairs = jnp.clip(plain_end // 2, 1, jnp.maximum(pairs, 1))
        alone = number == 1
        odd = (number > 1) & (lax.rem(number, 2) == 1)

        def looped(body):
            def step(i, carry):
                body(2 * i)
                return carry

            return step

        @pl.when(alone)
        def _():
            score(0, 1, True, True)

        @pl.when(jnp.logical_not(alone))
        def _():
            score(0, 2, True, True)

        lax.fori_loop(1, plain_pairs, looped(lambda j: score(j, 2, False, False)), 0)
        lax.fori_loop(plain_pairs, pairs, looped(lambda j: score(j, 2, True, False)), 0)

        @pl.when(odd)
        def _():
            score(number - 1, 1, True, False)

        for h in range(heads):
            best = jnp.max(top[h], axis=1, keepdims=True) * scale
            top[h] = jnp.broadcast_to(best, (BLOCK, 128))

        @pl.when(alone)
        def _():
            weigh(0, 1, True)

        @pl.when(jnp.logical_not(alone))
        def _():
            weigh(0, 2, True)

        lax.fori_loop(1, pairs, looped(lambda j: weigh(j, 2, False)), 0)

        @pl.when(odd)
        def _():
            weigh(number - 1, 1, False)

        for h in range(heads):
            rows = slice(h * BLOCK, (h + 1) * BLOCK)
            result = total[rows, :128] / total[rows, 128:]
            obuf[spans[slot], h * 128 : (h + 1) * 128] = result.astype(obuf.dtype)
        outs[slot].start()

    block(0)

    @pl.when(count == SLOTS)
    def _():
        block(1)

    @pl.when(count != SLOTS)
    def _():
        obuf[spans[1], :] = jnp.zeros((BLOCK, obuf.shape[1]), obuf.dtype)
        for h in range(heads):
            q_in[heads + h].wait()
        outs[1].start()

    for copy in outs:
        copy.wait()


def attend(lengths, counts, queries, kw, vw):
    heads = queries.shape[1] // 128
    entries = REACH + 2
    return pl.pallas_call(
        attend_kernel,
        out_shape=jax.ShapeDtypeStruct(queries.shape, jnp.bfloat16),
        in_specs=[
            pl.BlockSpec(memory_space=pltpu.SMEM),
            pl.BlockSpec(memory_space=pltpu.SMEM),
            pl.BlockSpec(memory_space=pl.ANY),
            pl.BlockSpec(memory_space=pl.ANY),
            pl.BlockSpec(memory_space=pl.ANY),
        ],
        out_specs=pl.BlockSpec(memory_space=pl.ANY),
        scratch_shapes=[
            pltpu.VMEM((SLOTS, heads * BLOCK, 128), jnp.bfloat16),
            pltpu.VMEM((entries, BLOCK, 128), jnp.bfloat16),
            pltpu.VMEM((entries, BLOCK, 128), jnp.bfloat16),
            pltpu.VMEM((REACH + 1, heads * BLOCK, BLOCK), jnp.float32),
            pltpu.VMEM((heads, BLOCK, 128), jnp.float32),
            pltpu.VMEM((heads * BLOCK, 256), jnp.float32),
            pltpu.VMEM((BLOCK, 128), jnp.int32),
            pltpu.VMEM(queries.shape, jnp.bfloat16),
            pltpu.SMEM((2 * REACH + 4,), jnp.int32),
            pltpu.SemaphoreType.DMA((2, entries)),
            pltpu.SemaphoreType.DMA((2, SLOTS * heads)),
        ],
        compiler_params=pltpu.CompilerParams(vmem_limit_bytes=60 * 2**20),
        name="attend",
    )(lengths, counts, queries, kw, vw)


def shards(queries, keys, values, doc_lengths, block_count):
    kw, vw = gather_windows(keys, values)
    return attend(doc_lengths, block_count, queries, kw, vw)


def solution(mesh):
    placed = (
        P(("outer", "inner"), "head"),
        P(("outer", "inner", "head"), None),
        P(("outer", "inner", "head"), None),
        P(),
        P(),
    )
    return jax.shard_map(
        shards, mesh=mesh, in_specs=placed, out_specs=P(("outer", "inner"), "head"), check_vma=False
    )
```

```python
import math

import jax
import jax.numpy as jnp
from jax import lax
from jax.experimental import pallas as pl
from jax.experimental.pallas import tpu as pltpu
from jax.sharding import PartitionSpec as P

BLOCK = 512
SLOTS = 2
REACH = 7
QUARTER = 256
LAYERS = 8
HALF = 128
MESH = pl.DeviceIdType.MESH
NEGATIVE = -1e30


def gather_kernel(k_ref, v_ref, kw, vw, send_sems, recv_sems, local_sems):
    outer = lax.axis_index("outer")
    inner = lax.axis_index("inner")
    y = lax.axis_index("head")
    z = outer * 2 + inner // 8
    x = lax.rem(inner // 2, 4)
    core = lax.rem(inner, 2)

    def place(px, py, pz, pc):
        return (pz // 2, lax.rem(pz, 2) * 8 + px * 2 + pc, py)

    xp, xm = lax.rem(x + 1, 4), lax.rem(x + 3, 4)
    yp, ym = lax.rem(y + 1, 4), lax.rem(y + 3, 4)
    zp, zm = lax.rem(z + 1, LAYERS), lax.rem(z + LAYERS - 1, LAYERS)
    z_next = jnp.where(x == 3, zp, z)
    z_prev = jnp.where(x == 0, zm, z)
    right, left = place(xp, y, z, core), place(xm, y, z, core)
    up, down = place(x, y, zp, core), place(x, y, zm, core)
    after, before = place(x, yp, z, core), place(x, ym, z, core)
    follower, leader = place(xp, y, z_next, core), place(xm, y, z_prev, core)
    sibling = place(x, y, z, 1 - core)

    chip = z * 4 + x
    last = LAYERS * 4 - 1
    has_up, has_down = z < LAYERS - 1, z > 0
    wanted = (x > 0) | (core == 1)
    barrier = pltpu.get_barrier_semaphore()

    def greet(partner):
        pl.semaphore_signal(barrier, inc=1, device_id=partner, device_id_type=MESH)

    for partner in (right, left, after, before, sibling):
        greet(partner)
    pl.when(has_up)(lambda: greet(up))
    pl.when(has_down)(lambda: greet(down))
    pl.when(chip < last)(lambda: greet(follower))
    pl.when(chip > 0)(lambda: greet(leader))

    def one(flag):
        return jnp.where(flag, 1, 0)

    partners = 5 + one(has_up) + one(has_down) + one(chip < last) + one(chip > 0)

    def present(name):
        if name[0] in ("k", "v"):
            return None if name[1] == 0 else chip >= name[1] // 2
        if name[0][1] == "u":
            return has_down & wanted
        return chip >= {"r": 1, "l": 3, "m": 2}[name[0][1]]

    def under(flag, run):
        if flag is None:
            run()
        else:
            pl.when(flag)(run)

    def rows(order, half=None):
        start = lax.rem(y + order, 4) * QUARTER
        if half is None:
            return pl.ds(pl.multiple_of(start, QUARTER), QUARTER)
        return pl.ds(pl.multiple_of(start + half * HALF, HALF), HALF)

    sems, arrived, sent = {}, set(), []

    def transfer(name, src, dst, device, arrives=None):
        sem = sems.setdefault(name, len(sems))
        end = sems.setdefault(arrives or name, len(sems))
        return pltpu.make_async_remote_copy(
            src_ref=src,
            dst_ref=dst,
            send_sem=send_sems.at[sem],
            recv_sem=recv_sems.at[end],
            device_id=device,
            device_id_type=MESH,
        )

    shapes = {}

    def post(name, src, dst, device, when=None, done=None, arrives=None, track=True):
        under(when, transfer(name, src, dst, device, arrives).start)
        shapes[name] = dst
        if track:
            sent.append((name, when if done is None else done))

    def finish(name, dst):
        return transfer(name, dst, dst, sibling)

    def need(*names):
        for name in names:
            if name not in arrived:
                arrived.add(name)
                under(present(name), finish(name, places[name]).wait_recv)

    places = {}
    for order in range(4):
        part = rows(order)
        places["ku", order] = kw.at[8, part]
        places["kr", order] = kw.at[2, part]
        places["kl", order] = kw.at[6, part]
        places["km", order] = kw.at[4, part]
    for half in range(2):
        part = rows(0, half)
        places["vu", half] = vw.at[8, part]
        places["vr", half] = vw.at[2, part]
        places["vl", half] = vw.at[6, part]
        places["vm", half] = vw.at[4, part]
    for win, ring, slots in ((kw, "k", (0,)), (vw, "v", (0, 2, 4, 6, 8))):
        for slot in slots:
            places[ring, slot, 0] = win.at[slot, rows(3)]
            places[ring, slot, 1] = win.at[slot, rows(1)]
            places[ring, slot, 2] = win.at[slot, rows(2, 0)]
            places[ring, slot, 3] = win.at[slot, rows(2, 1)]

    keep_k = pltpu.make_async_copy(k_ref, kw.at[0, rows(0)], local_sems.at[0])
    keep_v = pltpu.make_async_copy(v_ref, vw.at[0, rows(0)], local_sems.at[1])
    keep_k.start()
    keep_v.start()
    pl.semaphore_wait(barrier, partners)

    def key_open():
        post(("k", 0, 0), k_ref, kw.at[0, rows(0)], after)
        post(("k", 0, 1), k_ref, kw.at[0, rows(0)], before)

    def key_pass(side):
        need(("k", 0, side))
        part = rows((3, 1)[side], side)
        post(("k", 0, 2 + side), kw.at[0, part], kw.at[0, part], (after, before)[side])

    def send(kind, win, index, part, own):
        post((kind + "u", index), own, win.at[8, part], up, has_up & wanted)
        post((kind + "r", index), own, win.at[2, part], right, x < 3, (x < 3) | has_down)
        post((kind + "l", index), own, win.at[6, part], left, x == 0, (x == 0) | has_down)

    def turn(kind, win, index, part):
        need((kind + "u", index))
        post((kind + "r", index), win.at[8, part], win.at[2, part], right, (x == 3) & has_down, track=False)
        post((kind + "l", index), win.at[8, part], win.at[6, part], left, (x > 0) & has_down, track=False)

    def relay(kind, win, index, part, forward):
        name, there = (kind + "m", index), win.at[4, part]
        if forward:
            need((kind + "r", index))
            post(name, win.at[2, part], there, follower, (chip > 0) & (chip < last))
        else:
            need((kind + "l", index))
            post(name, win.at[6, part], there, leader, chip >= 3)
            need((kind + "r", index))
            post((kind + "x", index), win.at[2, part], there, follower, chip == last - 1, arrives=name)

    def key_send(order):
        if order == 3:
            need(("k", 0, 0))
        if order == 1:
            need(("k", 0, 1))
        if order == 2:
            need(("k", 0, 2), ("k", 0, 3))
        send("k", kw, order, rows(order), k_ref if order == 0 else kw.at[0, rows(order)])

    def key_turn(order):
        turn("k", kw, order, rows(order))

    def key_relay(order):
        relay("k", kw, order, rows(order), order in (0, 3))

    def value_send(half):
        send("v", vw, half, rows(0, half), v_ref.at[pl.ds(half * HALF, HALF)])

    def value_turn(half):
        turn("v", vw, half, rows(0, half))

    def value_relay(half):
        relay("v", vw, half, rows(0, half), half == 0)

    def only(slot, run):
        if slot == 8:
            pl.when((core == 1) & (chip >= 4))(run)
        elif slot:
            pl.when(chip >= slot // 2)(run)
        else:
            run()

    rings = []

    def ring_open(slot):
        if slot:
            source = {2: "vr", 4: "vm", 6: "vl", 8: "vu"}[slot]
            need((source, 0), (source, 1))
        own = vw.at[slot, rows(0)]

        def run():
            post(("v", slot, 0), own if slot else v_ref, own, after, track=False)
            post(("v", slot, 1), own if slot else v_ref, own, before, track=False)

        only(slot, run)
        rings.append(slot)

    def ring_pass(slot):
        parts = [vw.at[slot, rows(3, 0)], vw.at[slot, rows(1, 1)]]

        def run():
            for side, part in enumerate(parts):
                need(("v", slot, side))
                post(
                    ("v", slot, 2 + side),
                    part,
                    part,
                    (after, before)[side],
                    track=False,
                )

        only(slot, run)

    kept = []

    def keep():
        if not kept:
            kept.append(True)
            keep_k.wait()
            keep_v.wait()

    def share(win, slot):
        kind = "k" if win is kw else "v"
        if slot == 0:
            keep()
        if kind == "k" and slot:
            source = {2: "kr", 6: "kl", 8: "ku"}[slot]
            need(*((source, order) for order in range(4)))
        elif kind == "k":
            need(*(("k", 0, i) for i in range(4)))

        there = win.at[slot + 1 - 2 * core]
        if kind == "v":
            only(slot, lambda: need(*(("v", slot, i) for i in range(4))))
        name = (kind + "c", slot)
        if slot == 0:
            post(name, win.at[slot], there, sibling, core == 0)
        elif slot == 8:
            post(name, win.at[slot], there, sibling, core == 1)
        else:
            post(name, win.at[slot], there, sibling)

    def share_middle_keys(order):
        need(("km", order))
        part = rows(order)
        post(("kc", 4, order), kw.at[4, part], kw.at[5 - 2 * core, part], sibling)

    def share_middle_values(step):
        if step == 0:
            need(("vm", 0), ("vm", 1), ("v", 4, 0), ("v", 4, 1))
            parts = (0, 3, 1)
        else:
            need(("v", 4, 2), ("v", 4, 3))
            parts = (2,)
        for order in parts:
            part = rows(order)
            post(("vc", 4, order), vw.at[4, part], vw.at[5 - 2 * core, part], sibling)

    value_send(0)
    value_send(1)
    key_open()
    key_send(0)
    key_send(1)
    ring_open(0)
    value_turn(0)
    key_send(3)
    ring_open(8)
    value_turn(1)
    key_turn(0)
    key_pass(1)
    value_relay(0)
    key_pass(0)
    value_relay(1)
    ring_pass(0)
    key_turn(1)
    ring_pass(8)
    ring_open(2)
    key_send(2)
    ring_open(6)
    key_turn(3)
    key_turn(2)
    key_relay(0)
    share(vw, 0)
    ring_open(4)
    share(kw, 8)
    key_relay(1)
    share(vw, 8)
    ring_pass(6)
    key_relay(3)
    share(kw, 6)
    ring_pass(2)
    key_relay(2)
    ring_pass(4)
    share(kw, 0)
    share_middle_keys(1)
    share(kw, 2)
    share(vw, 6)
    share_middle_values(0)
    share_middle_keys(0)
    share(vw, 2)
    share_middle_keys(3)
    share_middle_values(1)
    share_middle_keys(2)
    keep()
    for kind, win in (("k", kw), ("v", vw)):
        for order in range(4):
            finish((kind + "c", 4, order), win.at[5, rows(order)]).wait_recv()
        for slot in (2, 6):
            finish((kind + "c", slot), win.at[slot]).wait_recv()
        pl.when(core == 1)(finish((kind + "c", 0), win.at[0]).wait_recv)
        pl.when(core == 0)(finish((kind + "c", 8), win.at[8]).wait_recv)

    for name, when in sent:
        under(when, finish(name, shapes[name]).wait_send)
    for slot in rings:

        def close(slot=slot):
            for i in range(4):
                finish(("v", slot, i), shapes["v", slot, i]).wait_send()

        only(slot, close)


def gather_windows(keys, values):
    depth = keys.shape[1]
    window = jax.ShapeDtypeStruct((REACH + 2, BLOCK * SLOTS, depth), keys.dtype)
    count = 112
    return pl.pallas_call(
        gather_kernel,
        out_shape=(window, window),
        in_specs=[pl.BlockSpec(memory_space=pl.ANY)] * 2,
        out_specs=(pl.BlockSpec(memory_space=pl.ANY),) * 2,
        scratch_shapes=[
            pltpu.SemaphoreType.DMA((count,)),
            pltpu.SemaphoreType.DMA((count,)),
            pltpu.SemaphoreType.DMA((2,)),
        ],
        compiler_params=pltpu.CompilerParams(collective_id=0, has_side_effects=True),
        name="gather_windows",
    )(keys, values)


def attend_kernel(
    lengths, counts, q_hbm, kw, vw, out_hbm, qbuf, kbuf, vbuf, scores, top, total, first, obuf, table, sems, io_sems
):
    heads = q_hbm.shape[1] // 128
    contexts = counts.shape[0]
    docs = lengths.shape[0]
    spans = [pl.ds(slot * BLOCK, BLOCK) for slot in range(SLOTS)]
    q_in = [
        pltpu.make_async_copy(
            q_hbm.at[spans[slot], h * 128 : (h + 1) * 128],
            qbuf.at[slot, pl.ds(h * BLOCK, BLOCK)],
            io_sems.at[0, slot * heads + h],
        )
        for slot in range(SLOTS)
        for h in range(heads)
    ]
    outs = [pltpu.make_async_copy(obuf.at[s], out_hbm.at[s], io_sems.at[1, i]) for i, s in enumerate(spans)]
    for copy in q_in:
        copy.start()

    me = lax.axis_index("outer") * 16 + lax.axis_index("inner")
    count = counts[me]
    before = jnp.int32(0)
    for i in range(contexts):
        before = before + jnp.where(i < me, counts[i], 0)
    base = before * BLOCK
    ends = []
    running = jnp.int32(0)
    for i in range(docs):
        running = running + lengths[i]
        ends.append(running)

    def start_of(position):
        best = jnp.int32(0)
        for end in ends:
            best = jnp.where(end <= position, end, best)
        return best

    table[0] = 1
    table[1] = 0
    filled = jnp.int32(2)
    for distance in range(1, REACH + 1):
        source = me - distance
        held = jnp.where(source >= 0, counts[jnp.maximum(source, 0)], 0)
        table[filled] = distance * SLOTS + held - 1
        table[filled + 1] = distance * SLOTS
        filled = filled + held

    lowest = start_of(base)
    needed = before - lowest // BLOCK + 1

    def fetch(entry, which):
        place = table[entry]
        window, buffer, sem = ((kw, kbuf, 0), (vw, vbuf, 1))[which]
        source = window.at[
            place // SLOTS, pl.ds(pl.multiple_of(lax.rem(place, SLOTS) * BLOCK, BLOCK), BLOCK)
        ]
        return pltpu.make_async_copy(source, buffer.at[entry], sems.at[sem, entry])

    for which in range(2):

        def one(i, carry):
            fetch(1 + i, which).start()
            return carry

        lax.fori_loop(0, needed, one, 0)

        @pl.when(count == SLOTS)
        def _():
            fetch(0, which).start()

    scale = math.log2(math.e) / math.sqrt(128)

    def block(slot):
        begin = base + slot * BLOCK
        low = lowest if slot == 0 else start_of(begin)
        high = start_of(begin + BLOCK - 1)
        number = (begin - low // BLOCK * BLOCK) // BLOCK + 1
        plain_end = jnp.maximum((begin - high) // BLOCK, 0) + 1
        position = begin + lax.broadcasted_iota(jnp.int32, (BLOCK, 128), 0)
        first[...] = jnp.full((BLOCK, 128), low, jnp.int32)

        def mark(i, running):
            @pl.when((running > begin) & (running < begin + BLOCK))
            def _():
                first[...] = jnp.where(position >= running, running, first[...])

            return running + lengths[i]

        @pl.when(high != low)
        def _():
            lax.fori_loop(0, docs, mark, jnp.int32(0))

        for h in range(heads):
            q_in[slot * heads + h].wait()

        def wait_for(j, width, which):
            if slot == 0:
                for step in range(width):
                    fetch(1 + j + step, which).wait()
            elif isinstance(j, int) and j == 0:
                fetch(0, which).wait()

        def score(j, width, masked, fresh):
            entry = 1 - slot + j
            wait_for(j, width, 0)
            product = lax.dot_general(
                qbuf[slot],
                kbuf[pl.ds(entry, width)].reshape(width * BLOCK, 128),
                (((1,), (1,)), ((), ())),
                preferred_element_type=jnp.float32,
            )
            best = [None if fresh else top[h] for h in range(heads)]
            for step in range(width):
                for part in range(BLOCK // 128):
                    if masked:
                        key = (
                            begin
                            - (j + step) * BLOCK
                            + part * 128
                            + lax.broadcasted_iota(jnp.int32, (BLOCK, 128), 1)
                        )
                        mask = (key >= first[...]) & (key <= position)
                    for h in range(heads):
                        rows = slice(h * BLOCK, (h + 1) * BLOCK)
                        piece = product[rows, step * BLOCK + part * 128 : step * BLOCK + (part + 1) * 128]
                        if masked:
                            piece = jnp.where(mask, piece, NEGATIVE)
                        scores[j + step, rows, part * 128 : (part + 1) * 128] = piece
                        best[h] = piece if best[h] is None else jnp.maximum(best[h], piece)
            for h in range(heads):
                top[h] = best[h]

        def weigh(j, width, fresh):
            entry = 1 - slot + j
            wait_for(j, width, 1)
            value = vbuf[pl.ds(entry, width)].reshape(width * BLOCK, 128)
            widened = jnp.concatenate([value, jnp.ones_like(value)], axis=1)
            highest = top[...].reshape(heads * BLOCK, 128)
            weights = []
            for step in range(width):
                for part in range(BLOCK // 128):
                    shifted = scores[j + step, :, part * 128 : (part + 1) * 128] * scale - highest
                    weights.append(jnp.exp2(shifted).astype(jnp.bfloat16))
            product = jnp.dot(
                jnp.concatenate(weights, axis=1), widened, preferred_element_type=jnp.float32
            )
            if fresh:
                total[...] = product
            else:
                total[...] += product

        pairs = number // 2
        plain_pairs = jnp.clip(plain_end // 2, 1, jnp.maximum(pairs, 1))
        alone = number == 1
        odd = (number > 1) & (lax.rem(number, 2) == 1)

        def looped(body):
            def step(i, carry):
                body(2 * i)
                return carry

            return step

        @pl.when(alone)
        def _():
            score(0, 1, True, True)

        @pl.when(jnp.logical_not(alone))
        def _():
            score(0, 2, True, True)

        lax.fori_loop(1, plain_pairs, looped(lambda j: score(j, 2, False, False)), 0)
        lax.fori_loop(plain_pairs, pairs, looped(lambda j: score(j, 2, True, False)), 0)

        @pl.when(odd)
        def _():
            score(number - 1, 1, True, False)

        for h in range(heads):
            best = jnp.max(top[h], axis=1, keepdims=True) * scale
            top[h] = jnp.broadcast_to(best, (BLOCK, 128))

        @pl.when(alone)
        def _():
            weigh(0, 1, True)

        @pl.when(jnp.logical_not(alone))
        def _():
            weigh(0, 2, True)

        lax.fori_loop(1, pairs, looped(lambda j: weigh(j, 2, False)), 0)

        @pl.when(odd)
        def _():
            weigh(number - 1, 1, False)

        for h in range(heads):
            rows = slice(h * BLOCK, (h + 1) * BLOCK)
            result = total[rows, :128] / total[rows, 128:]
            obuf[spans[slot], h * 128 : (h + 1) * 128] = result.astype(obuf.dtype)
        outs[slot].start()

    block(0)

    @pl.when(count == SLOTS)
    def _():
        block(1)

    @pl.when(count != SLOTS)
    def _():
        obuf[spans[1], :] = jnp.zeros((BLOCK, obuf.shape[1]), obuf.dtype)
        for h in range(heads):
            q_in[heads + h].wait()
        outs[1].start()

    for copy in outs:
        copy.wait()


def attend(lengths, counts, queries, kw, vw):
    heads = queries.shape[1] // 128
    entries = REACH + 2
    return pl.pallas_call(
        attend_kernel,
        out_shape=jax.ShapeDtypeStruct(queries.shape, jnp.bfloat16),
        in_specs=[
            pl.BlockSpec(memory_space=pltpu.SMEM),
            pl.BlockSpec(memory_space=pltpu.SMEM),
            pl.BlockSpec(memory_space=pl.ANY),
            pl.BlockSpec(memory_space=pl.ANY),
            pl.BlockSpec(memory_space=pl.ANY),
        ],
        out_specs=pl.BlockSpec(memory_space=pl.ANY),
        scratch_shapes=[
            pltpu.VMEM((SLOTS, heads * BLOCK, 128), jnp.bfloat16),
            pltpu.VMEM((entries, BLOCK, 128), jnp.bfloat16),
            pltpu.VMEM((entries, BLOCK, 128), jnp.bfloat16),
            pltpu.VMEM((REACH + 1, heads * BLOCK, BLOCK), jnp.float32),
            pltpu.VMEM((heads, BLOCK, 128), jnp.float32),
            pltpu.VMEM((heads * BLOCK, 256), jnp.float32),
            pltpu.VMEM((BLOCK, 128), jnp.int32),
            pltpu.VMEM(queries.shape, jnp.bfloat16),
            pltpu.SMEM((2 * REACH + 4,), jnp.int32),
            pltpu.SemaphoreType.DMA((2, entries)),
            pltpu.SemaphoreType.DMA((2, SLOTS * heads)),
        ],
        compiler_params=pltpu.CompilerParams(vmem_limit_bytes=60 * 2**20),
        name="attend",
    )(lengths, counts, queries, kw, vw)


def shards(queries, keys, values, doc_lengths, block_count):
    kw, vw = gather_windows(keys, values)
    return attend(doc_lengths, block_count, queries, kw, vw)


def solution(mesh):
    placed = (
        P(("outer", "inner"), "head"),
        P(("outer", "inner", "head"), None),
        P(("outer", "inner", "head"), None),
        P(),
        P(),
    )
    return jax.shard_map(
        shards, mesh=mesh, in_specs=placed, out_specs=P(("outer", "inner"), "head"), check_vma=False
    )
```

```python
import math

import jax
import jax.numpy as jnp
from jax import lax
from jax.experimental import pallas as pl
from jax.experimental.pallas import tpu as pltpu
from jax.sharding import PartitionSpec as P

BLOCK = 512
SLOTS = 2
REACH = 7
QUARTER = 256
LAYERS = 8
HALF = 128
MESH = pl.DeviceIdType.MESH
NEGATIVE = -1e30


def gather_kernel(k_ref, v_ref, kw, vw, send_sems, recv_sems, local_sems):
    outer = lax.axis_index("outer")
    inner = lax.axis_index("inner")
    y = lax.axis_index("head")
    z = outer * 2 + inner // 8
    x = lax.rem(inner // 2, 4)
    core = lax.rem(inner, 2)

    def place(px, py, pz, pc):
        return (pz // 2, lax.rem(pz, 2) * 8 + px * 2 + pc, py)

    xp, xm = lax.rem(x + 1, 4), lax.rem(x + 3, 4)
    yp, ym = lax.rem(y + 1, 4), lax.rem(y + 3, 4)
    zp, zm = lax.rem(z + 1, LAYERS), lax.rem(z + LAYERS - 1, LAYERS)
    z_next = jnp.where(x == 3, zp, z)
    z_prev = jnp.where(x == 0, zm, z)
    right, left = place(xp, y, z, core), place(xm, y, z, core)
    up, down = place(x, y, zp, core), place(x, y, zm, core)
    after, before = place(x, yp, z, core), place(x, ym, z, core)
    follower, leader = place(xp, y, z_next, core), place(xm, y, z_prev, core)
    sibling = place(x, y, z, 1 - core)

    chip = z * 4 + x
    last = LAYERS * 4 - 1
    has_up, has_down = z < LAYERS - 1, z > 0
    wanted = (x > 0) | (core == 1)
    barrier = pltpu.get_barrier_semaphore()

    def greet(partner):
        pl.semaphore_signal(barrier, inc=1, device_id=partner, device_id_type=MESH)

    for partner in (right, left, after, before, sibling):
        greet(partner)
    pl.when(has_up)(lambda: greet(up))
    pl.when(has_down)(lambda: greet(down))
    pl.when(chip < last)(lambda: greet(follower))
    pl.when(chip > 0)(lambda: greet(leader))

    def one(flag):
        return jnp.where(flag, 1, 0)

    partners = 5 + one(has_up) + one(has_down) + one(chip < last) + one(chip > 0)

    def present(name):
        if name[0] in ("k", "v"):
            return None if name[1] == 0 else chip >= name[1] // 2
        if name[0][1] == "u":
            return has_down & wanted
        return chip >= {"r": 1, "l": 3, "m": 2}[name[0][1]]

    def under(flag, run):
        if flag is None:
            run()
        else:
            pl.when(flag)(run)

    def rows(order, half=None):
        start = lax.rem(y + order, 4) * QUARTER
        if half is None:
            return pl.ds(pl.multiple_of(start, QUARTER), QUARTER)
        return pl.ds(pl.multiple_of(start + half * HALF, HALF), HALF)

    sems, arrived, sent = {}, set(), []

    def transfer(name, src, dst, device, arrives=None):
        sem = sems.setdefault(name, len(sems))
        end = sems.setdefault(arrives or name, len(sems))
        return pltpu.make_async_remote_copy(
            src_ref=src,
            dst_ref=dst,
            send_sem=send_sems.at[sem],
            recv_sem=recv_sems.at[end],
            device_id=device,
            device_id_type=MESH,
        )

    shapes = {}

    def post(name, src, dst, device, when=None, done=None, arrives=None, track=True):
        under(when, transfer(name, src, dst, device, arrives).start)
        shapes[name] = dst
        if track:
            sent.append((name, when if done is None else done))

    def finish(name, dst):
        return transfer(name, dst, dst, sibling)

    def need(*names):
        for name in names:
            if name not in arrived:
                arrived.add(name)
                under(present(name), finish(name, places[name]).wait_recv)

    places = {}
    for order in range(4):
        part = rows(order)
        places["ku", order] = kw.at[8, part]
        places["kr", order] = kw.at[2, part]
        places["kl", order] = kw.at[6, part]
        places["km", order] = kw.at[4, part]
    for half in range(2):
        part = rows(0, half)
        places["vu", half] = vw.at[8, part]
        places["vr", half] = vw.at[2, part]
        places["vl", half] = vw.at[6, part]
        places["vm", half] = vw.at[4, part]
    for win, ring, slots in ((kw, "k", (0,)), (vw, "v", (0, 2, 4, 6, 8))):
        for slot in slots:
            places[ring, slot, 0] = win.at[slot, rows(3)]
            places[ring, slot, 1] = win.at[slot, rows(1)]
            places[ring, slot, 2] = win.at[slot, rows(2, 0)]
            places[ring, slot, 3] = win.at[slot, rows(2, 1)]

    keep_k = pltpu.make_async_copy(k_ref, kw.at[0, rows(0)], local_sems.at[0])
    keep_v = pltpu.make_async_copy(v_ref, vw.at[0, rows(0)], local_sems.at[1])
    keep_k.start()
    keep_v.start()
    pl.semaphore_wait(barrier, partners)

    def key_open():
        post(("k", 0, 0), k_ref, kw.at[0, rows(0)], after)
        post(("k", 0, 1), k_ref, kw.at[0, rows(0)], before)

    def key_pass(side):
        need(("k", 0, side))
        part = rows((3, 1)[side], side)
        post(("k", 0, 2 + side), kw.at[0, part], kw.at[0, part], (after, before)[side])

    def send(kind, win, index, part, own):
        post((kind + "u", index), own, win.at[8, part], up, has_up & wanted)
        post((kind + "r", index), own, win.at[2, part], right, x < 3, (x < 3) | has_down)
        post((kind + "l", index), own, win.at[6, part], left, x == 0, (x == 0) | has_down)

    def turn(kind, win, index, part):
        need((kind + "u", index))
        post((kind + "r", index), win.at[8, part], win.at[2, part], right, (x == 3) & has_down, track=False)
        post((kind + "l", index), win.at[8, part], win.at[6, part], left, (x > 0) & has_down, track=False)

    def relay(kind, win, index, part, forward):
        name, there = (kind + "m", index), win.at[4, part]
        if forward:
            need((kind + "r", index))
            post(name, win.at[2, part], there, follower, (chip > 0) & (chip < last))
        else:
            need((kind + "l", index))
            post(name, win.at[6, part], there, leader, chip >= 3)
            need((kind + "r", index))
            post((kind + "x", index), win.at[2, part], there, follower, chip == last - 1, arrives=name)

    def key_send(order):
        if order == 3:
            need(("k", 0, 0))
        if order == 1:
            need(("k", 0, 1))
        if order == 2:
            need(("k", 0, 2), ("k", 0, 3))
        send("k", kw, order, rows(order), k_ref if order == 0 else kw.at[0, rows(order)])

    def key_turn(order):
        turn("k", kw, order, rows(order))

    def key_relay(order):
        relay("k", kw, order, rows(order), order in (0, 3))

    def value_send(half):
        send("v", vw, half, rows(0, half), v_ref.at[pl.ds(half * HALF, HALF)])

    def value_turn(half):
        turn("v", vw, half, rows(0, half))

    def value_relay(half):
        relay("v", vw, half, rows(0, half), half == 0)

    def only(slot, run):
        if slot == 8:
            pl.when((core == 1) & (chip >= 4))(run)
        elif slot:
            pl.when(chip >= slot // 2)(run)
        else:
            run()

    rings = []

    def ring_open(slot):
        if slot:
            source = {2: "vr", 4: "vm", 6: "vl", 8: "vu"}[slot]
            need((source, 0), (source, 1))
        own = vw.at[slot, rows(0)]

        def run():
            post(("v", slot, 0), own if slot else v_ref, own, after, track=False)
            post(("v", slot, 1), own if slot else v_ref, own, before, track=False)

        only(slot, run)
        rings.append(slot)

    def ring_pass(slot):
        parts = [vw.at[slot, rows(3, 0)], vw.at[slot, rows(1, 1)]]

        def run():
            for side, part in enumerate(parts):
                need(("v", slot, side))
                post(
                    ("v", slot, 2 + side),
                    part,
                    part,
                    (after, before)[side],
                    track=False,
                )

        only(slot, run)

    kept = []

    def keep():
        if not kept:
            kept.append(True)
            keep_k.wait()
            keep_v.wait()

    def share(win, slot):
        kind = "k" if win is kw else "v"
        if slot == 0:
            keep()
        if kind == "k" and slot:
            source = {2: "kr", 6: "kl", 8: "ku"}[slot]
            need(*((source, order) for order in range(4)))
        elif kind == "k":
            need(*(("k", 0, i) for i in range(4)))

        there = win.at[slot + 1 - 2 * core]
        if kind == "v":
            only(slot, lambda: need(*(("v", slot, i) for i in range(4))))
        name = (kind + "c", slot)
        if slot == 0:
            post(name, win.at[slot], there, sibling, core == 0)
        elif slot == 8:
            post(name, win.at[slot], there, sibling, core == 1)
        else:
            post(name, win.at[slot], there, sibling)

    def share_middle_keys(order):
        need(("km", order))
        part = rows(order)
        post(("kc", 4, order), kw.at[4, part], kw.at[5 - 2 * core, part], sibling)

    def share_middle_values(step):
        if step == 0:
            need(("vm", 0), ("vm", 1), ("v", 4, 0), ("v", 4, 1))
            parts = (0, 3, 1)
        else:
            need(("v", 4, 2), ("v", 4, 3))
            parts = (2,)
        for order in parts:
            part = rows(order)
            post(("vc", 4, order), vw.at[4, part], vw.at[5 - 2 * core, part], sibling)

    value_send(0)
    value_send(1)
    key_open()
    key_send(0)
    key_send(1)
    ring_open(0)
    value_turn(0)
    key_send(3)
    ring_open(8)
    value_turn(1)
    key_turn(0)
    key_pass(1)
    value_relay(0)
    key_pass(0)
    value_relay(1)
    ring_pass(0)
    key_turn(1)
    ring_pass(8)
    ring_open(2)
    key_send(2)
    ring_open(6)
    key_turn(3)
    key_turn(2)
    key_relay(0)
    share(vw, 0)
    ring_open(4)
    share(kw, 8)
    key_relay(1)
    share(vw, 8)
    ring_pass(6)
    key_relay(3)
    share(kw, 6)
    ring_pass(2)
    key_relay(2)
    ring_pass(4)
    share(kw, 0)
    share_middle_keys(1)
    share(kw, 2)
    share(vw, 6)
    share_middle_values(0)
    share_middle_keys(0)
    share(vw, 2)
    share_middle_keys(3)
    share_middle_values(1)
    share_middle_keys(2)
    keep()
    for kind, win in (("k", kw), ("v", vw)):
        for order in range(4):
            finish((kind + "c", 4, order), win.at[5, rows(order)]).wait_recv()
        for slot in (2, 6):
            finish((kind + "c", slot), win.at[slot]).wait_recv()
        pl.when(core == 1)(finish((kind + "c", 0), win.at[0]).wait_recv)
        pl.when(core == 0)(finish((kind + "c", 8), win.at[8]).wait_recv)

    for name, when in sent:
        under(when, finish(name, shapes[name]).wait_send)
    for slot in rings:

        def close(slot=slot):
            for i in range(4):
                finish(("v", slot, i), shapes["v", slot, i]).wait_send()

        only(slot, close)


def gather_windows(keys, values):
    depth = keys.shape[1]
    window = jax.ShapeDtypeStruct((REACH + 2, BLOCK * SLOTS, depth), keys.dtype)
    count = 112
    return pl.pallas_call(
        gather_kernel,
        out_shape=(window, window),
        in_specs=[pl.BlockSpec(memory_space=pl.ANY)] * 2,
        out_specs=(pl.BlockSpec(memory_space=pl.ANY),) * 2,
        scratch_shapes=[
            pltpu.SemaphoreType.DMA((count,)),
            pltpu.SemaphoreType.DMA((count,)),
            pltpu.SemaphoreType.DMA((2,)),
        ],
        compiler_params=pltpu.CompilerParams(collective_id=0, has_side_effects=True),
        name="gather_windows",
    )(keys, values)


def attend_kernel(
    lengths, counts, q_hbm, kw, vw, out_hbm, qbuf, kbuf, vbuf, scores, top, total, first, obuf, table, sems, io_sems
):
    heads = q_hbm.shape[1] // 128
    contexts = counts.shape[0]
    docs = lengths.shape[0]
    spans = [pl.ds(slot * BLOCK, BLOCK) for slot in range(SLOTS)]
    q_in = [
        pltpu.make_async_copy(
            q_hbm.at[spans[slot], h * 128 : (h + 1) * 128],
            qbuf.at[slot, pl.ds(h * BLOCK, BLOCK)],
            io_sems.at[0, slot * heads + h],
        )
        for slot in range(SLOTS)
        for h in range(heads)
    ]
    outs = [pltpu.make_async_copy(obuf.at[s], out_hbm.at[s], io_sems.at[1, i]) for i, s in enumerate(spans)]
    for copy in q_in:
        copy.start()

    me = lax.axis_index("outer") * 16 + lax.axis_index("inner")
    count = counts[me]
    before = jnp.int32(0)
    for i in range(contexts):
        before = before + jnp.where(i < me, counts[i], 0)
    base = before * BLOCK
    ends = []
    running = jnp.int32(0)
    for i in range(docs):
        running = running + lengths[i]
        ends.append(running)

    def start_of(position):
        best = jnp.int32(0)
        for end in ends:
            best = jnp.where(end <= position, end, best)
        return best

    table[0] = 1
    table[1] = 0
    filled = jnp.int32(2)
    for distance in range(1, REACH + 1):
        source = me - distance
        held = jnp.where(source >= 0, counts[jnp.maximum(source, 0)], 0)
        table[filled] = distance * SLOTS + held - 1
        table[filled + 1] = distance * SLOTS
        filled = filled + held

    lowest = start_of(base)
    needed = before - lowest // BLOCK + 1

    def fetch(entry, which):
        place = table[entry]
        window, buffer, sem = ((kw, kbuf, 0), (vw, vbuf, 1))[which]
        source = window.at[
            place // SLOTS, pl.ds(pl.multiple_of(lax.rem(place, SLOTS) * BLOCK, BLOCK), BLOCK)
        ]
        return pltpu.make_async_copy(source, buffer.at[entry], sems.at[sem, entry])

    for which in range(2):

        def one(i, carry):
            fetch(1 + i, which).start()
            return carry

        lax.fori_loop(0, needed, one, 0)

        @pl.when(count == SLOTS)
        def _():
            fetch(0, which).start()

    scale = math.log2(math.e) / math.sqrt(128)

    def block(slot):
        begin = base + slot * BLOCK
        low = lowest if slot == 0 else start_of(begin)
        high = start_of(begin + BLOCK - 1)
        number = (begin - low // BLOCK * BLOCK) // BLOCK + 1
        plain_end = jnp.maximum((begin - high) // BLOCK, 0) + 1
        position = begin + lax.broadcasted_iota(jnp.int32, (BLOCK, 128), 0)
        first[...] = jnp.full((BLOCK, 128), low, jnp.int32)

        def mark(i, running):
            @pl.when((running > begin) & (running < begin + BLOCK))
            def _():
                first[...] = jnp.where(position >= running, running, first[...])

            return running + lengths[i]

        @pl.when(high != low)
        def _():
            lax.fori_loop(0, docs, mark, jnp.int32(0))

        for h in range(heads):
            q_in[slot * heads + h].wait()

        def wait_for(j, width, which):
            if slot == 0:
                for step in range(width):
                    fetch(1 + j + step, which).wait()
            elif isinstance(j, int) and j == 0:
                fetch(0, which).wait()

        def score(j, width, masked, fresh):
            entry = 1 - slot + j
            wait_for(j, width, 0)
            product = lax.dot_general(
                qbuf[slot],
                kbuf[pl.ds(entry, width)].reshape(width * BLOCK, 128),
                (((1,), (1,)), ((), ())),
                preferred_element_type=jnp.float32,
            )
            best = [None if fresh else top[h] for h in range(heads)]
            for step in range(width):
                for part in range(BLOCK // 128):
                    if masked:
                        key = (
                            begin
                            - (j + step) * BLOCK
                            + part * 128
                            + lax.broadcasted_iota(jnp.int32, (BLOCK, 128), 1)
                        )
                        mask = (key >= first[...]) & (key <= position)
                    for h in range(heads):
                        rows = slice(h * BLOCK, (h + 1) * BLOCK)
                        piece = product[rows, step * BLOCK + part * 128 : step * BLOCK + (part + 1) * 128]
                        if masked:
                            piece = jnp.where(mask, piece, NEGATIVE)
                        scores[j + step, rows, part * 128 : (part + 1) * 128] = piece
                        best[h] = piece if best[h] is None else jnp.maximum(best[h], piece)
            for h in range(heads):
                top[h] = best[h]

        def weigh(j, width, fresh):
            entry = 1 - slot + j
            wait_for(j, width, 1)
            value = vbuf[pl.ds(entry, width)].reshape(width * BLOCK, 128)
            widened = jnp.concatenate([value, jnp.ones_like(value)], axis=1)
            highest = top[...].reshape(heads * BLOCK, 128)
            weights = []
            for step in range(width):
                for part in range(BLOCK // 128):
                    shifted = scores[j + step, :, part * 128 : (part + 1) * 128] * scale - highest
                    weights.append(jnp.exp2(shifted).astype(jnp.bfloat16))
            product = jnp.dot(
                jnp.concatenate(weights, axis=1), widened, preferred_element_type=jnp.float32
            )
            if fresh:
                total[...] = product
            else:
                total[...] += product

        pairs = number // 2
        many = number >= 4
        few = (number > 1) & (number < 4)
        begin_pairs = jnp.where(many, 2, 1)
        plain_pairs = jnp.clip(plain_end // 2, begin_pairs, jnp.maximum(pairs, begin_pairs))
        alone = number == 1
        odd = (number > 1) & (lax.rem(number, 2) == 1)

        def looped(body):
            def step(i, carry):
                body(2 * i)
                return carry

            return step

        @pl.when(alone)
        def _():
            score(0, 1, True, True)

        @pl.when(few)
        def _():
            score(0, 2, True, True)

        @pl.when(many)
        def _():
            score(0, 4, True, True)

        lax.fori_loop(begin_pairs, plain_pairs, looped(lambda j: score(j, 2, False, False)), 0)
        lax.fori_loop(plain_pairs, pairs, looped(lambda j: score(j, 2, True, False)), 0)

        @pl.when(odd)
        def _():
            score(number - 1, 1, True, False)

        for h in range(heads):
            best = jnp.max(top[h], axis=1, keepdims=True) * scale
            top[h] = jnp.broadcast_to(best, (BLOCK, 128))

        @pl.when(alone)
        def _():
            weigh(0, 1, True)

        @pl.when(few)
        def _():
            weigh(0, 2, True)

        @pl.when(many)
        def _():
            weigh(0, 4, True)

        lax.fori_loop(begin_pairs, pairs, looped(lambda j: weigh(j, 2, False)), 0)

        @pl.when(odd)
        def _():
            weigh(number - 1, 1, False)

        for h in range(heads):
            rows = slice(h * BLOCK, (h + 1) * BLOCK)
            result = total[rows, :128] / total[rows, 128:]
            obuf[spans[slot], h * 128 : (h + 1) * 128] = result.astype(obuf.dtype)
        outs[slot].start()

    block(0)

    @pl.when(count == SLOTS)
    def _():
        block(1)

    @pl.when(count != SLOTS)
    def _():
        obuf[spans[1], :] = jnp.zeros((BLOCK, obuf.shape[1]), obuf.dtype)
        for h in range(heads):
            q_in[heads + h].wait()
        outs[1].start()

    for copy in outs:
        copy.wait()


def attend(lengths, counts, queries, kw, vw):
    heads = queries.shape[1] // 128
    entries = REACH + 2
    return pl.pallas_call(
        attend_kernel,
        out_shape=jax.ShapeDtypeStruct(queries.shape, jnp.bfloat16),
        in_specs=[
            pl.BlockSpec(memory_space=pltpu.SMEM),
            pl.BlockSpec(memory_space=pltpu.SMEM),
            pl.BlockSpec(memory_space=pl.ANY),
            pl.BlockSpec(memory_space=pl.ANY),
            pl.BlockSpec(memory_space=pl.ANY),
        ],
        out_specs=pl.BlockSpec(memory_space=pl.ANY),
        scratch_shapes=[
            pltpu.VMEM((SLOTS, heads * BLOCK, 128), jnp.bfloat16),
            pltpu.VMEM((entries, BLOCK, 128), jnp.bfloat16),
            pltpu.VMEM((entries, BLOCK, 128), jnp.bfloat16),
            pltpu.VMEM((REACH + 1, heads * BLOCK, BLOCK), jnp.float32),
            pltpu.VMEM((heads, BLOCK, 128), jnp.float32),
            pltpu.VMEM((heads * BLOCK, 256), jnp.float32),
            pltpu.VMEM((BLOCK, 128), jnp.int32),
            pltpu.VMEM(queries.shape, jnp.bfloat16),
            pltpu.SMEM((2 * REACH + 4,), jnp.int32),
            pltpu.SemaphoreType.DMA((2, entries)),
            pltpu.SemaphoreType.DMA((2, SLOTS * heads)),
        ],
        compiler_params=pltpu.CompilerParams(vmem_limit_bytes=60 * 2**20),
        name="attend",
    )(lengths, counts, queries, kw, vw)


def shards(queries, keys, values, doc_lengths, block_count):
    kw, vw = gather_windows(keys, values)
    return attend(doc_lengths, block_count, queries, kw, vw)


def solution(mesh):
    placed = (
        P(("outer", "inner"), "head"),
        P(("outer", "inner", "head"), None),
        P(("outer", "inner", "head"), None),
        P(),
        P(),
    )
    return jax.shard_map(
        shards, mesh=mesh, in_specs=placed, out_specs=P(("outer", "inner"), "head"), check_vma=False
    )
```

```python
import math

import jax
import jax.numpy as jnp
from jax import lax
from jax.experimental import pallas as pl
from jax.experimental.pallas import tpu as pltpu
from jax.sharding import PartitionSpec as P

BLOCK = 512
SLOTS = 2
REACH = 7
QUARTER = 256
LAYERS = 8
HALF = 128
MESH = pl.DeviceIdType.MESH
NEGATIVE = -1e30


def gather_kernel(k_ref, v_ref, kw, vw, send_sems, recv_sems, local_sems):
    outer = lax.axis_index("outer")
    inner = lax.axis_index("inner")
    y = lax.axis_index("head")
    z = outer * 2 + inner // 8
    x = lax.rem(inner // 2, 4)
    core = lax.rem(inner, 2)

    def place(px, py, pz, pc):
        return (pz // 2, lax.rem(pz, 2) * 8 + px * 2 + pc, py)

    xp, xm = lax.rem(x + 1, 4), lax.rem(x + 3, 4)
    yp, ym = lax.rem(y + 1, 4), lax.rem(y + 3, 4)
    zp, zm = lax.rem(z + 1, LAYERS), lax.rem(z + LAYERS - 1, LAYERS)
    z_next = jnp.where(x == 3, zp, z)
    z_prev = jnp.where(x == 0, zm, z)
    right, left = place(xp, y, z, core), place(xm, y, z, core)
    up, down = place(x, y, zp, core), place(x, y, zm, core)
    after, before = place(x, yp, z, core), place(x, ym, z, core)
    follower, leader = place(xp, y, z_next, core), place(xm, y, z_prev, core)
    sibling = place(x, y, z, 1 - core)

    chip = z * 4 + x
    last = LAYERS * 4 - 1
    has_up, has_down = z < LAYERS - 1, z > 0
    wanted = (x > 0) | (core == 1)
    barrier = pltpu.get_barrier_semaphore()

    def greet(partner):
        pl.semaphore_signal(barrier, inc=1, device_id=partner, device_id_type=MESH)

    for partner in (right, left, after, before, sibling):
        greet(partner)
    pl.when(has_up)(lambda: greet(up))
    pl.when(has_down)(lambda: greet(down))
    pl.when(chip < last)(lambda: greet(follower))
    pl.when(chip > 0)(lambda: greet(leader))

    def one(flag):
        return jnp.where(flag, 1, 0)

    partners = 5 + one(has_up) + one(has_down) + one(chip < last) + one(chip > 0)

    def present(name):
        if name[0] in ("k", "v"):
            return None if name[1] == 0 else chip >= name[1] // 2
        if name[0][1] == "u":
            return has_down & wanted
        return chip >= {"r": 1, "l": 3, "m": 2}[name[0][1]]

    def under(flag, run):
        if flag is None:
            run()
        else:
            pl.when(flag)(run)

    def rows(order, half=None):
        start = lax.rem(y + order, 4) * QUARTER
        if half is None:
            return pl.ds(pl.multiple_of(start, QUARTER), QUARTER)
        return pl.ds(pl.multiple_of(start + half * HALF, HALF), HALF)

    sems, arrived, sent = {}, set(), []

    def transfer(name, src, dst, device, arrives=None):
        sem = sems.setdefault(name, len(sems))
        end = sems.setdefault(arrives or name, len(sems))
        return pltpu.make_async_remote_copy(
            src_ref=src,
            dst_ref=dst,
            send_sem=send_sems.at[sem],
            recv_sem=recv_sems.at[end],
            device_id=device,
            device_id_type=MESH,
        )

    shapes, early = {}, set()

    def post(name, src, dst, device, when=None, done=None, arrives=None, track=True):
        under(when, transfer(name, src, dst, device, arrives).start)
        shapes[name] = dst
        if track:
            sent.append((name, when if done is None else done))

    def finish(name, dst):
        return transfer(name, dst, dst, sibling)

    def need(*names):
        for name in names:
            if name not in arrived:
                arrived.add(name)
                flag = present(name)
                if name in early:
                    flag = flag & (chip != last - 1)
                under(flag, finish(name, places[name]).wait_recv)

    places = {}
    for order in range(4):
        part = rows(order)
        places["ku", order] = kw.at[8, part]
        places["kr", order] = kw.at[2, part]
        places["kl", order] = kw.at[6, part]
        places["km", order] = kw.at[4, part]
    for half in range(2):
        part = rows(0, half)
        places["vu", half] = vw.at[8, part]
        places["vr", half] = vw.at[2, part]
        places["vl", half] = vw.at[6, part]
        places["vm", half] = vw.at[4, part]
    for win, ring, slots in ((kw, "k", (0,)), (vw, "v", (0, 2, 4, 6, 8))):
        for slot in slots:
            places[ring, slot, 0] = win.at[slot, rows(3)]
            places[ring, slot, 1] = win.at[slot, rows(1)]
            places[ring, slot, 2] = win.at[slot, rows(2, 0)]
            places[ring, slot, 3] = win.at[slot, rows(2, 1)]

    keep_k = pltpu.make_async_copy(k_ref, kw.at[0, rows(0)], local_sems.at[0])
    keep_v = pltpu.make_async_copy(v_ref, vw.at[0, rows(0)], local_sems.at[1])
    keep_k.start()
    keep_v.start()
    pl.semaphore_wait(barrier, partners)

    def key_open():
        post(("k", 0, 0), k_ref, kw.at[0, rows(0)], after)
        post(("k", 0, 1), k_ref, kw.at[0, rows(0)], before)

    def key_pass(side):
        need(("k", 0, side))
        part = rows((3, 1)[side], side)
        post(("k", 0, 2 + side), kw.at[0, part], kw.at[0, part], (after, before)[side])

    def send(kind, win, index, part, own):
        post((kind + "u", index), own, win.at[8, part], up, has_up & wanted)
        post((kind + "r", index), own, win.at[2, part], right, x < 3, (x < 3) | has_down)
        post((kind + "l", index), own, win.at[6, part], left, x == 0, (x == 0) | has_down)

    def turn(kind, win, index, part):
        need((kind + "u", index))
        post((kind + "r", index), win.at[8, part], win.at[2, part], right, (x == 3) & has_down, track=False)
        post((kind + "l", index), win.at[8, part], win.at[6, part], left, (x > 0) & has_down, track=False)

    def relay(kind, win, index, part, forward):
        name, there = (kind + "m", index), win.at[4, part]
        if forward:
            need((kind + "r", index))
            post(name, win.at[2, part], there, follower, (chip > 0) & (chip < last))
        else:
            need((kind + "l", index))
            post(name, win.at[6, part], there, leader, chip >= 3)
            source = (kind + "r", index)
            if source not in arrived:
                early.add(source)
                pl.when(chip == last - 1)(finish(source, places[source]).wait_recv)
            post((kind + "x", index), win.at[2, part], there, follower, chip == last - 1, arrives=name)

    def key_send(order):
        if order == 3:
            need(("k", 0, 0))
        if order == 1:
            need(("k", 0, 1))
        if order == 2:
            need(("k", 0, 2), ("k", 0, 3))
        send("k", kw, order, rows(order), k_ref if order == 0 else kw.at[0, rows(order)])

    def key_turn(order):
        turn("k", kw, order, rows(order))

    def key_relay(order):
        relay("k", kw, order, rows(order), order in (0, 3))

    def value_send(half):
        send("v", vw, half, rows(0, half), v_ref.at[pl.ds(half * HALF, HALF)])

    def value_turn(half):
        turn("v", vw, half, rows(0, half))

    def value_relay(half):
        relay("v", vw, half, rows(0, half), half == 0)

    def only(slot, run):
        if slot == 8:
            pl.when((core == 1) & (chip >= 4))(run)
        elif slot:
            pl.when(chip >= slot // 2)(run)
        else:
            run()

    rings = []

    def ring_open(slot):
        if slot:
            source = {2: "vr", 4: "vm", 6: "vl", 8: "vu"}[slot]
            need((source, 0), (source, 1))
        own = vw.at[slot, rows(0)]

        def run():
            post(("v", slot, 0), own if slot else v_ref, own, after, track=False)
            post(("v", slot, 1), own if slot else v_ref, own, before, track=False)

        only(slot, run)
        rings.append(slot)

    def ring_pass(slot):
        parts = [vw.at[slot, rows(3, 0)], vw.at[slot, rows(1, 1)]]

        def run():
            for side, part in enumerate(parts):
                need(("v", slot, side))
                post(
                    ("v", slot, 2 + side),
                    part,
                    part,
                    (after, before)[side],
                    track=False,
                )

        only(slot, run)

    kept = []

    def keep():
        if not kept:
            kept.append(True)
            keep_k.wait()
            keep_v.wait()

    def share(win, slot):
        kind = "k" if win is kw else "v"
        if slot == 0:
            keep()
        if kind == "k" and slot:
            source = {2: "kr", 6: "kl", 8: "ku"}[slot]
            need(*((source, order) for order in range(4)))
        elif kind == "k":
            need(*(("k", 0, i) for i in range(4)))

        there = win.at[slot + 1 - 2 * core]
        if kind == "v":
            only(slot, lambda: need(*(("v", slot, i) for i in range(4))))
        name = (kind + "c", slot)
        if slot == 0:
            post(name, win.at[slot], there, sibling, core == 0)
        elif slot == 8:
            post(name, win.at[slot], there, sibling, core == 1)
        else:
            post(name, win.at[slot], there, sibling)

    def share_middle_keys(order):
        need(("km", order))
        part = rows(order)
        post(("kc", 4, order), kw.at[4, part], kw.at[5 - 2 * core, part], sibling)

    def share_middle_values(step):
        if step == 0:
            need(("vm", 0), ("vm", 1), ("v", 4, 0), ("v", 4, 1))
            parts = (0, 3, 1)
        else:
            need(("v", 4, 2), ("v", 4, 3))
            parts = (2,)
        for order in parts:
            part = rows(order)
            post(("vc", 4, order), vw.at[4, part], vw.at[5 - 2 * core, part], sibling)

    value_send(0)
    value_send(1)
    key_open()
    key_send(0)
    key_send(1)
    ring_open(0)
    value_turn(0)
    key_send(3)
    ring_open(8)
    value_turn(1)
    key_turn(0)
    key_pass(1)
    value_relay(0)
    key_pass(0)
    value_relay(1)
    ring_pass(0)
    key_turn(1)
    ring_pass(8)
    ring_open(2)
    key_send(2)
    ring_open(6)
    key_turn(3)
    key_turn(2)
    key_relay(0)
    share(vw, 0)
    ring_open(4)
    share(kw, 8)
    key_relay(1)
    share(vw, 8)
    ring_pass(6)
    key_relay(3)
    share(kw, 6)
    ring_pass(2)
    key_relay(2)
    ring_pass(4)
    share(kw, 0)
    share_middle_keys(1)
    share(kw, 2)
    share(vw, 6)
    share_middle_values(0)
    share_middle_keys(0)
    share(vw, 2)
    share_middle_keys(3)
    share_middle_values(1)
    share_middle_keys(2)
    keep()
    for kind, win in (("k", kw), ("v", vw)):
        for order in range(4):
            finish((kind + "c", 4, order), win.at[5, rows(order)]).wait_recv()
        for slot in (2, 6):
            finish((kind + "c", slot), win.at[slot]).wait_recv()
        pl.when(core == 1)(finish((kind + "c", 0), win.at[0]).wait_recv)
        pl.when(core == 0)(finish((kind + "c", 8), win.at[8]).wait_recv)

    for name, when in sent:
        under(when, finish(name, shapes[name]).wait_send)
    for slot in rings:

        def close(slot=slot):
            for i in range(4):
                finish(("v", slot, i), shapes["v", slot, i]).wait_send()

        only(slot, close)


def gather_windows(keys, values):
    depth = keys.shape[1]
    window = jax.ShapeDtypeStruct((REACH + 2, BLOCK * SLOTS, depth), keys.dtype)
    count = 112
    return pl.pallas_call(
        gather_kernel,
        out_shape=(window, window),
        in_specs=[pl.BlockSpec(memory_space=pl.ANY)] * 2,
        out_specs=(pl.BlockSpec(memory_space=pl.ANY),) * 2,
        scratch_shapes=[
            pltpu.SemaphoreType.DMA((count,)),
            pltpu.SemaphoreType.DMA((count,)),
            pltpu.SemaphoreType.DMA((2,)),
        ],
        compiler_params=pltpu.CompilerParams(collective_id=0, has_side_effects=True),
        name="gather_windows",
    )(keys, values)


def attend_kernel(
    lengths, counts, q_hbm, kw, vw, out_hbm, qbuf, kbuf, vbuf, scores, top, total, first, obuf, table, sems, io_sems
):
    heads = q_hbm.shape[1] // 128
    contexts = counts.shape[0]
    docs = lengths.shape[0]
    spans = [pl.ds(slot * BLOCK, BLOCK) for slot in range(SLOTS)]
    q_in = [
        pltpu.make_async_copy(
            q_hbm.at[spans[slot], h * 128 : (h + 1) * 128],
            qbuf.at[slot, pl.ds(h * BLOCK, BLOCK)],
            io_sems.at[0, slot * heads + h],
        )
        for slot in range(SLOTS)
        for h in range(heads)
    ]
    outs = [pltpu.make_async_copy(obuf.at[s], out_hbm.at[s], io_sems.at[1, i]) for i, s in enumerate(spans)]
    for copy in q_in:
        copy.start()

    me = lax.axis_index("outer") * 16 + lax.axis_index("inner")
    count = counts[me]
    before = jnp.int32(0)
    for i in range(contexts):
        before = before + jnp.where(i < me, counts[i], 0)
    base = before * BLOCK
    ends = []
    running = jnp.int32(0)
    for i in range(docs):
        running = running + lengths[i]
        ends.append(running)

    def start_of(position):
        best = jnp.int32(0)
        for end in ends:
            best = jnp.where(end <= position, end, best)
        return best

    table[0] = 1
    table[1] = 0
    filled = jnp.int32(2)
    for distance in range(1, REACH + 1):
        source = me - distance
        held = jnp.where(source >= 0, counts[jnp.maximum(source, 0)], 0)
        table[filled] = distance * SLOTS + held - 1
        table[filled + 1] = distance * SLOTS
        filled = filled + held

    lowest = start_of(base)
    needed = before - lowest // BLOCK + 1

    def fetch(entry, which):
        place = table[entry]
        window, buffer, sem = ((kw, kbuf, 0), (vw, vbuf, 1))[which]
        source = window.at[
            place // SLOTS, pl.ds(pl.multiple_of(lax.rem(place, SLOTS) * BLOCK, BLOCK), BLOCK)
        ]
        return pltpu.make_async_copy(source, buffer.at[entry], sems.at[sem, entry])

    for which in range(2):

        def one(i, carry):
            fetch(1 + i, which).start()
            return carry

        lax.fori_loop(0, needed, one, 0)

        @pl.when(count == SLOTS)
        def _():
            fetch(0, which).start()

    scale = math.log2(math.e) / math.sqrt(128)

    def block(slot):
        begin = base + slot * BLOCK
        low = lowest if slot == 0 else start_of(begin)
        high = start_of(begin + BLOCK - 1)
        number = (begin - low // BLOCK * BLOCK) // BLOCK + 1
        plain_end = jnp.maximum((begin - high) // BLOCK, 0) + 1
        position = begin + lax.broadcasted_iota(jnp.int32, (BLOCK, 128), 0)
        first[...] = jnp.full((BLOCK, 128), low, jnp.int32)

        def mark(i, running):
            @pl.when((running > begin) & (running < begin + BLOCK))
            def _():
                first[...] = jnp.where(position >= running, running, first[...])

            return running + lengths[i]

        @pl.when(high != low)
        def _():
            lax.fori_loop(0, docs, mark, jnp.int32(0))

        for h in range(heads):
            q_in[slot * heads + h].wait()

        def wait_for(j, width, which):
            if slot == 0:
                for step in range(width):
                    fetch(1 + j + step, which).wait()
            elif isinstance(j, int) and j == 0:
                fetch(0, which).wait()

        def score(j, width, masked, fresh):
            entry = 1 - slot + j
            wait_for(j, width, 0)
            product = lax.dot_general(
                qbuf[slot],
                kbuf[pl.ds(entry, width)].reshape(width * BLOCK, 128),
                (((1,), (1,)), ((), ())),
                preferred_element_type=jnp.float32,
            )
            best = [None if fresh else top[h] for h in range(heads)]
            for step in range(width):
                for part in range(BLOCK // 128):
                    if masked:
                        key = (
                            begin
                            - (j + step) * BLOCK
                            + part * 128
                            + lax.broadcasted_iota(jnp.int32, (BLOCK, 128), 1)
                        )
                        mask = (key >= first[...]) & (key <= position)
                    for h in range(heads):
                        rows = slice(h * BLOCK, (h + 1) * BLOCK)
                        piece = product[rows, step * BLOCK + part * 128 : step * BLOCK + (part + 1) * 128]
                        if masked:
                            piece = jnp.where(mask, piece, NEGATIVE)
                        scores[j + step, rows, part * 128 : (part + 1) * 128] = piece
                        best[h] = piece if best[h] is None else jnp.maximum(best[h], piece)
            for h in range(heads):
                top[h] = best[h]

        def weigh(j, width, fresh):
            entry = 1 - slot + j
            wait_for(j, width, 1)
            value = vbuf[pl.ds(entry, width)].reshape(width * BLOCK, 128)
            widened = jnp.concatenate([value, jnp.ones_like(value)], axis=1)
            highest = top[...].reshape(heads * BLOCK, 128)
            weights = []
            for step in range(width):
                for part in range(BLOCK // 128):
                    shifted = scores[j + step, :, part * 128 : (part + 1) * 128] * scale - highest
                    weights.append(jnp.exp2(shifted).astype(jnp.bfloat16))
            product = jnp.dot(
                jnp.concatenate(weights, axis=1), widened, preferred_element_type=jnp.float32
            )
            if fresh:
                total[...] = product
            else:
                total[...] += product

        pairs = number // 2
        plain_pairs = jnp.clip(plain_end // 2, 1, jnp.maximum(pairs, 1))
        alone = number == 1
        odd = (number > 1) & (lax.rem(number, 2) == 1)

        def looped(body):
            def step(i, carry):
                body(2 * i)
                return carry

            return step

        @pl.when(alone)
        def _():
            score(0, 1, True, True)

        @pl.when(jnp.logical_not(alone))
        def _():
            score(0, 2, True, True)

        lax.fori_loop(1, plain_pairs, looped(lambda j: score(j, 2, False, False)), 0)
        lax.fori_loop(plain_pairs, pairs, looped(lambda j: score(j, 2, True, False)), 0)

        @pl.when(odd)
        def _():
            score(number - 1, 1, True, False)

        for h in range(heads):
            best = jnp.max(top[h], axis=1, keepdims=True) * scale
            top[h] = jnp.broadcast_to(best, (BLOCK, 128))

        @pl.when(alone)
        def _():
            weigh(0, 1, True)

        @pl.when(jnp.logical_not(alone))
        def _():
            weigh(0, 2, True)

        lax.fori_loop(1, pairs, looped(lambda j: weigh(j, 2, False)), 0)

        @pl.when(odd)
        def _():
            weigh(number - 1, 1, False)

        for h in range(heads):
            rows = slice(h * BLOCK, (h + 1) * BLOCK)
            result = total[rows, :128] / total[rows, 128:]
            obuf[spans[slot], h * 128 : (h + 1) * 128] = result.astype(obuf.dtype)
        outs[slot].start()

    block(0)

    @pl.when(count == SLOTS)
    def _():
        block(1)

    @pl.when(count != SLOTS)
    def _():
        obuf[spans[1], :] = jnp.zeros((BLOCK, obuf.shape[1]), obuf.dtype)
        for h in range(heads):
            q_in[heads + h].wait()
        outs[1].start()

    for copy in outs:
        copy.wait()


def attend(lengths, counts, queries, kw, vw):
    heads = queries.shape[1] // 128
    entries = REACH + 2
    return pl.pallas_call(
        attend_kernel,
        out_shape=jax.ShapeDtypeStruct(queries.shape, jnp.bfloat16),
        in_specs=[
            pl.BlockSpec(memory_space=pltpu.SMEM),
            pl.BlockSpec(memory_space=pltpu.SMEM),
            pl.BlockSpec(memory_space=pl.ANY),
            pl.BlockSpec(memory_space=pl.ANY),
            pl.BlockSpec(memory_space=pl.ANY),
        ],
        out_specs=pl.BlockSpec(memory_space=pl.ANY),
        scratch_shapes=[
            pltpu.VMEM((SLOTS, heads * BLOCK, 128), jnp.bfloat16),
            pltpu.VMEM((entries, BLOCK, 128), jnp.bfloat16),
            pltpu.VMEM((entries, BLOCK, 128), jnp.bfloat16),
            pltpu.VMEM((REACH + 1, heads * BLOCK, BLOCK), jnp.float32),
            pltpu.VMEM((heads, BLOCK, 128), jnp.float32),
            pltpu.VMEM((heads * BLOCK, 256), jnp.float32),
            pltpu.VMEM((BLOCK, 128), jnp.int32),
            pltpu.VMEM(queries.shape, jnp.bfloat16),
            pltpu.SMEM((2 * REACH + 4,), jnp.int32),
            pltpu.SemaphoreType.DMA((2, entries)),
            pltpu.SemaphoreType.DMA((2, SLOTS * heads)),
        ],
        compiler_params=pltpu.CompilerParams(vmem_limit_bytes=60 * 2**20),
        name="attend",
    )(lengths, counts, queries, kw, vw)


def shards(queries, keys, values, doc_lengths, block_count):
    kw, vw = gather_windows(keys, values)
    return attend(doc_lengths, block_count, queries, kw, vw)


def solution(mesh):
    placed = (
        P(("outer", "inner"), "head"),
        P(("outer", "inner", "head"), None),
        P(("outer", "inner", "head"), None),
        P(),
        P(),
    )
    return jax.shard_map(
        shards, mesh=mesh, in_specs=placed, out_specs=P(("outer", "inner"), "head"), check_vma=False
    )
```
